32 devices in a mesh: grp: 2 (over y), row: 8 (over z, x), col: 2 (over core).
Axes of the slice: x: 2, y: 2, z: 4, core: 2. Of those that a mesh axis runs over, the one named last changes fastest.
Arguments:
- features: bfloat16 [128, 128, 256], P(('grp', 'row'), 'col'), parts along dimension 0, may hold values from -6 to 6
- cotangent: bfloat16 [128, 128, 256], P(('grp', 'row'), 'col'), parts along dimension 0, may hold values from -6 to 6
- domain: int32 [128, 128], P(('grp', 'row'), 'col'), parts along dimension 0, may hold values 0 or 1
- qkv_weight: bfloat16 [256, 768], replicated, may hold values from -6 to 6
- proj_weight: bfloat16 [256, 256], replicated, may hold values from -0.375 to 0.375
- norm_gain: float32 [256], replicated, may hold values from 0.5 to 1.5
Outputs:
- updated: bfloat16 [128, 128, 256], P(('grp', 'row'), 'col'), parts along dimension 0
- grad_features: bfloat16 [128, 128, 256], P(('grp', 'row'), 'col'), parts along dimension 0
- grad_qkv: float32 [512, 768], P('grp'), parts along dimension 0
- grad_proj: float32 [512, 256], P('grp'), parts along dimension 0
- grad_gain: float32 [512], P('grp'), parts along dimension 0
The draws below stay inside these ranges and needn't reach their ends.
There are 2 independent parts, one for each index of `grp`. The reference program is written for one: setup_inputs(seed, part) draws one part's arguments, and reference() takes and returns one part's arrays. A program takes and returns all parts, laid end to end along the dimension named above; an argument that names none is the same for every part. Nothing has to cross between parts.
All inputs are finite; a program needn't handle non-finite values. No bound on the sum of `domain` on one device may be relied on, other than what follows from the above.
Results may differ from the reference program's by a relative error of at most 0.013.
Values may be sent and summed in bfloat16 or wider, within the bound.
A program may use at most 64 MiB of HBM per device.

```python
import jax
import jax.numpy as jnp
from jax import lax

D = 256
HEADS = 8
WIN = 8
SHIFT = 4
HEIGHT = 64
WIDTH = 128


def draw_qkv_weight(key, part):
    return (jax.random.normal(key, (D, 3 * D), jnp.float32) * D ** (-0.5)).astype(jnp.bfloat16)


def touch_ends(drawn, key, low, high):
    longest = drawn.shape.index(max(drawn.shape))
    spots = []
    for shift in (0, 1):
        where = [jax.random.randint(jax.random.fold_in(key, axis), (), 0, length) for axis, length in enumerate(drawn.shape)]
        where[longest] = (where[longest] + shift) % drawn.shape[longest]
        spots.append(tuple(where))
    return drawn.at[spots[0]].set(low).at[spots[1]].set(high)


def levels(own_key, shape, shards, least, high):
    level, own = 1.0, jax.random.fold_in(own_key, 6)
    for axis_at, blocks in shards:
        heights = jnp.exp(jax.random.uniform(jax.random.fold_in(own, axis_at), (blocks,), jnp.float32, least / len(shards), high / len(shards)))
        level = level * jnp.repeat(heights, shape[axis_at] // blocks).reshape([-1 if axis == axis_at else 1 for axis in range(len(shape))])
    return level


def noise(stream_key, dims, width, reach, cuts=(), kind=jnp.bfloat16):
    factor_of = levels(stream_key, dims, cuts, -0.22, 0.18) if cuts else 1.0
    drawn = jax.random.normal(stream_key, dims, jnp.float32) * width * factor_of
    return jnp.minimum(jnp.maximum(drawn, -reach), reach).astype(kind)


def setup_inputs(seed: int = 0, part: int = 0) -> dict:
    splits = jax.random.split(jax.random.key(seed), 7)
    part_keys = jax.random.split(jax.random.fold_in(splits[6], part), 7)
    features = noise(part_keys[0], (HEIGHT, WIDTH, D), 1.0, 6.0, ((0, 8), (1, 2)))
    cotangent = noise(part_keys[1], (HEIGHT, WIDTH, D), 1.0, 6.0, ((0, 8), (1, 2)))
    domain = touch_ends((jax.random.randint(part_keys[2], (HEIGHT, WIDTH), 0, 4) < 3).astype(jnp.int32), jax.random.fold_in(part_keys[2], 1), 0, 1)
    qkv_weight = draw_qkv_weight(jax.random.fold_in(splits[6], 71), part)
    proj_weight = noise(splits[4], (D, D), D ** -0.5, 0.375)
    norm_gain = jnp.clip(1.0 + 0.1 * jax.random.normal(splits[5], (D,), jnp.float32), 0.5, 1.5)
    return dict(features=features, cotangent=cotangent, domain=domain, qkv_weight=qkv_weight, proj_weight=proj_weight, norm_gain=norm_gain)


NORM_EPSILON = 1e-05
MASKED_SCORE = -1e+30

def layer_norm(values, norm_gain):
    average = lax.optimization_barrier(jnp.mean(values, -1, keepdims=True))
    centred = values - average
    variance = lax.optimization_barrier(jnp.mean(centred * centred, -1, keepdims=True))
    return centred * lax.rsqrt(variance + NORM_EPSILON) * norm_gain

def region_of(cell_ids, extent):
    return (cell_ids >= extent - WIN).astype(jnp.int32) + (cell_ids >= extent - SHIFT).astype(jnp.int32)

def region_labels(row_start, tile_rows, total_rows, col_start, tile_cols, total_cols):
    row_ids = row_start + jnp.arange(tile_rows, dtype=jnp.int32)
    col_ids = col_start + jnp.arange(tile_cols, dtype=jnp.int32)
    return region_of(row_ids, total_rows)[:, None] * 3 + region_of(col_ids, total_cols)[None, :]

def contract_rows(left, right):
    return lax.dot_general(left, right, (((0,), (0,)), ((), ())), preferred_element_type=jnp.float32)

def contract_cols(left, right):
    return lax.dot_general(left, right, (((1,), (1,)), ((), ())), preferred_element_type=jnp.float32)

def window_core(projected, labels):
    tile_rows, tile_cols, triple = projected.shape
    channels = triple // 3
    windows = tile_cols // WIN
    head_dim = channels // HEADS
    grouped = projected.reshape(tile_rows, windows, WIN, triple).transpose(1, 0, 2, 3).reshape(windows, tile_rows * WIN, triple)
    grouped_labels = labels.reshape(tile_rows, windows, WIN).transpose(1, 0, 2).reshape(windows, tile_rows * WIN)
    query_part = grouped[:, :, :channels].reshape(windows, -1, HEADS, head_dim)
    key_part = grouped[:, :, channels:2 * channels].reshape(windows, -1, HEADS, head_dim)
    value_part = grouped[:, :, 2 * channels:].reshape(windows, -1, HEADS, head_dim)
    scores = jnp.einsum('wqhd,wkhd->whqk', query_part, key_part) * head_dim ** (-0.5)
    allowed = (grouped_labels[:, :, None] == grouped_labels[:, None, :])[:, None]
    scores = jnp.where(allowed, scores, MASKED_SCORE)
    peak = lax.stop_gradient(lax.optimization_barrier(jnp.max(scores, -1, keepdims=True)))
    weights = jnp.exp(scores - peak)
    probability = weights / lax.optimization_barrier(jnp.sum(weights, -1, keepdims=True))
    probability = lax.optimization_barrier(probability.astype(jnp.bfloat16)).astype(jnp.float32)
    context = jnp.einsum('whqk,wkhd->wqhd', probability, value_part)
    context = context.reshape(windows, tile_rows, WIN, channels).transpose(1, 0, 2, 3).reshape(tile_rows, tile_cols, channels)
    return context.astype(jnp.bfloat16)

def forward_block(shifted, labels, qkv_weight, proj_weight):
    tile_rows, tile_cols, channels = shifted.shape
    flat_rows = shifted.reshape(-1, channels)
    projected = jnp.dot(flat_rows, qkv_weight, preferred_element_type=jnp.float32).astype(jnp.bfloat16)
    projected = projected.reshape(tile_rows, tile_cols, 3 * channels)
    context = window_core(projected.astype(jnp.float32), labels)
    attended = jnp.dot(context.reshape(-1, channels), proj_weight, preferred_element_type=jnp.float32).astype(jnp.bfloat16)
    return (projected, context, attended.reshape(shifted.shape))

def backward_block(shifted, labels, projected, context, dattended, qkv_weight, proj_weight):
    channels = shifted.shape[-1]
    grad_rows = dattended.reshape(-1, channels)
    grad_proj = contract_rows(context.reshape(-1, channels), grad_rows)
    dcontext = contract_cols(grad_rows, proj_weight).astype(jnp.bfloat16).reshape(context.shape)

    def core_only(values):
        return window_core(values, labels)
    _, pullback = jax.vjp(core_only, projected.astype(jnp.float32))
    dprojected = pullback(dcontext)[0].astype(jnp.bfloat16).reshape(-1, 3 * channels)
    grad_qkv = contract_rows(shifted.reshape(-1, channels), dprojected)
    dshifted = contract_cols(dprojected, qkv_weight).astype(jnp.bfloat16).reshape(shifted.shape)
    return (grad_qkv, grad_proj, dshifted)

def norm_backward(values, norm_gain, dnormed):

    def apply_norm(inputs):
        return layer_norm(inputs, norm_gain)
    _, pullback = jax.vjp(apply_norm, values)
    upstream = dnormed.astype(jnp.float32)
    grad_values = pullback(upstream)[0]
    standard = layer_norm(values, jnp.ones_like(norm_gain))
    grad_gain = lax.optimization_barrier(jnp.sum((upstream * standard).reshape(-1, values.shape[-1]), 0))
    return (grad_values, grad_gain)

def reference(features, cotangent, domain, qkv_weight, proj_weight, norm_gain):
    total_rows, total_cols, channels = features.shape
    values = features.astype(jnp.float32)
    normed = layer_norm(values, norm_gain).astype(jnp.bfloat16)
    shifted = jnp.roll(normed, (-SHIFT, -SHIFT), (0, 1))
    labels = region_labels(0, total_rows, total_rows, 0, total_cols, total_cols)
    bands = shifted.reshape(total_rows // WIN, WIN, total_cols, channels)
    band_labels = labels.reshape(total_rows // WIN, WIN, total_cols)

    def forward_step(inputs):
        return forward_block(inputs[0], inputs[1], qkv_weight, proj_weight)[2]
    attended = lax.map(forward_step, (bands, band_labels)).reshape(total_rows, total_cols, channels)
    inside = domain.astype(jnp.float32)[..., None]
    updated = (values + inside * jnp.roll(attended, (SHIFT, SHIFT), (0, 1)).astype(jnp.float32)).astype(jnp.bfloat16)
    masked_grad = cotangent * domain.astype(jnp.bfloat16)[..., None]
    dattended = jnp.roll(masked_grad, (-SHIFT, -SHIFT), (0, 1)).reshape(bands.shape)

    def backward_step(totals, inputs):
        band, tags, grad_band = inputs
        projected, context, _ = forward_block(band, tags, qkv_weight, proj_weight)
        part_qkv, part_proj, dshifted = backward_block(band, tags, projected, context, grad_band, qkv_weight, proj_weight)
        return ((totals[0] + part_qkv, totals[1] + part_proj), dshifted)
    zeros_init = (jnp.zeros((channels, 3 * channels), jnp.float32), jnp.zeros((channels, channels), jnp.float32))
    (grad_qkv, grad_proj), dshifted = lax.scan(backward_step, zeros_init, (bands, band_labels, dattended))
    dnormed = jnp.roll(dshifted.reshape(total_rows, total_cols, channels), (SHIFT, SHIFT), (0, 1))
    grad_values, grad_gain = norm_backward(values, norm_gain, dnormed)
    grad_features = (cotangent.astype(jnp.float32) + grad_values).astype(jnp.bfloat16)
    return (updated, grad_features, grad_qkv, grad_proj, grad_gain)
```

```python
import functools

import jax
import jax.numpy as jnp
from jax import lax
from jax.experimental import pallas as pl
from jax.experimental.pallas import tpu as pltpu
from jax.sharding import PartitionSpec as P

HEADS = 8
WIN = 8
SHIFT = 4
NORM_EPSILON = 1e-05
MASKED_SCORE = -1e30
LOG2E = 1.4426950408889634
INNER = 8
PAD = 16

F32 = jnp.float32
BF16 = jnp.bfloat16


def nn(a, b):
    return lax.dot_general(a, b, (((1,), (0,)), ((), ())), preferred_element_type=F32)


def nt(a, b):
    return lax.dot_general(a, b, (((1,), (1,)), ((), ())), preferred_element_type=F32)


def tn(a, b):
    return lax.dot_general(a, b, (((0,), (0,)), ((), ())), preferred_element_type=F32)


def kernel(
    rows,
    cols,
    feat_ref,
    cot_ref,
    dom_ref,
    wqkv_ref,
    wproj_ref,
    gain_ref,
    upd_ref,
    gfeat_ref,
    gsum_ref,
    ggain_ref,
    ext_f,
    ext_c,
    ext_d,
    xf,
    cf,
    dx,
    mask,
    xhat,
    rstd,
    shifted,
    datt,
    proj,
    dproj,
    ctx,
    dctx,
    out32,
    outx,
    row_in,
    col_in,
    diag_in,
    part,
    core_out,
    core_in,
    gcore_out,
    gcore_in,
    sbuf,
    rbuf,
    obuf,
    oin,
    in_send,
    in_recv,
    out_send,
    out_recv,
    core_send,
    core_recv,
    rs_send,
    rs_recv,
    o_send,
    o_recv,
    ag_send,
    ag_recv,
    fw_send,
    fw_recv,
):
    tile_rows, tile_cols, channels = feat_ref.shape
    windows = tile_cols // WIN
    cells = WIN * WIN
    head_dim = channels // HEADS
    outer = rows // INNER
    me_r = lax.axis_index("row")
    me_c = lax.axis_index("col")
    r_up = lax.rem(me_r + rows - 1, rows)
    r_dn = lax.rem(me_r + 1, rows)
    c_left = lax.rem(me_c + cols - 1, cols)
    c_right = lax.rem(me_c + 1, cols)
    group = me_r // INNER
    member = lax.rem(me_r, INNER)

    def dev(r, c):
        return {"row": r, "col": c}

    def peer(o):
        return group * INNER + lax.rem(member + o, INNER)

    def counterpart(o):
        return lax.rem(group + o, outer) * INNER + member

    barrier = pltpu.get_barrier_semaphore()
    greeted = [
        dev(r_up, me_c),
        dev(r_dn, me_c),
        dev(me_r, c_left),
        dev(r_up, c_left),
        dev(r_dn, c_right),
    ]
    greeted += [dev(peer(o), me_c) for o in range(1, INNER)]
    greeted += [dev(counterpart(o), me_c) for o in range(1, outer)]
    for target in greeted:
        pl.semaphore_signal(barrier, inc=1, device_id=target, device_id_type=pl.DeviceIdType.MESH)
    pl.semaphore_wait(barrier, len(greeted))

    def remote(src, dst, send, recv, target):
        return pltpu.make_async_remote_copy(
            src_ref=src,
            dst_ref=dst,
            send_sem=send,
            recv_sem=recv,
            device_id=target,
            device_id_type=pl.DeviceIdType.MESH,
        )

    up, left, corner = dev(r_up, me_c), dev(me_r, c_left), dev(r_up, c_left)
    top, low = pl.ds(0, SHIFT), pl.ds(SHIFT, SHIFT)
    body, side = pl.ds(0, tile_cols), pl.ds(tile_cols, PAD)
    head = pl.ds(0, PAD)
    jobs = []
    for src, dst in ((feat_ref, ext_f), (cot_ref, ext_c)):
        jobs.append((src.at[top], dst.at[low, body], up))
        jobs.append((src.at[low, head], dst.at[top, side], left))
        jobs.append((src.at[top, head], dst.at[low, side], corner))
    for i, target in enumerate((up, left, corner)):
        jobs.append((dom_ref, ext_d.at[i], target))
    halos = [
        remote(s, d, in_send.at[i], in_recv.at[i], t) for i, (s, d, t) in enumerate(jobs)
    ]
    for copy in halos:
        copy.start()
    out32[:, :, 0:8, :] = jnp.zeros((2, tile_rows, 8, channels), F32)
    out32[:, :, tile_cols : tile_cols + PAD, :] = jnp.zeros((2, tile_rows, PAD, channels), F32)
    xf[0:SHIFT, 0:tile_cols, :] = feat_ref[SHIFT:, :, :].astype(F32)
    cf[0:SHIFT, 0:tile_cols, :] = cot_ref[SHIFT:, :, :].astype(F32)
    for copy in halos:
        copy.wait()
    xf[SHIFT:, 0:tile_cols, :] = ext_f[SHIFT:, 0:tile_cols, :].astype(F32)
    cf[SHIFT:, 0:tile_cols, :] = ext_c[SHIFT:, 0:tile_cols, :].astype(F32)
    xf[:, tile_cols:, :] = ext_f[:, tile_cols:, :].astype(F32)
    cf[:, tile_cols:, :] = ext_c[:, tile_cols:, :].astype(F32)

    lane = lax.broadcasted_iota(jnp.int32, (SHIFT, 2 * tile_cols), 1)
    dx[0:SHIFT, :] = jnp.where(lane < tile_cols, dom_ref[SHIFT:, :], ext_d[1, SHIFT:, :])
    dx[SHIFT:, :] = jnp.where(lane < tile_cols, ext_d[0, 0:SHIFT, :], ext_d[2, 0:SHIFT, :])
    pick = lax.broadcasted_iota(jnp.int32, (WIN, 2 * tile_cols), 1) - lax.broadcasted_iota(
        jnp.int32, (WIN, 2 * tile_cols), 0
    )
    for i in range(tile_rows):
        line = jnp.broadcast_to(dx[i : i + 1, :], (WIN, 2 * tile_cols))
        for w in range(windows):
            mask[w, i * WIN : (i + 1) * WIN, :] = jnp.sum(
                jnp.where(pick == w * WIN + SHIFT, line, 0.0), -1, keepdims=True
            )

    gain = gain_ref[...]
    for w in range(windows):
        at = slice(w * WIN + SHIFT, (w + 1) * WIN + SHIFT)
        x = xf[:, at, :].reshape(cells, channels)
        average = jnp.mean(x, -1, keepdims=True)
        centred = x - average
        variance = jnp.mean(centred * centred, -1, keepdims=True)
        inv = lax.rsqrt(variance + NORM_EPSILON)
        standard = centred * inv
        rstd[w] = inv
        xhat[w] = standard
        shifted[w] = (standard * gain).astype(BF16)
        c = cf[:, at, :].reshape(cells, channels)
        datt[w] = (c * mask[w]).astype(BF16)

    total = windows * cells
    flat_s = shifted[...].reshape(total, channels)
    flat_d = datt[...].reshape(total, channels)
    proj[...] = nn(flat_s, wqkv_ref[...]).astype(BF16).reshape(windows, cells, 3 * channels)
    dctx[...] = nt(flat_d, wproj_ref[...]).astype(BF16).reshape(windows, cells, channels)

    scale = head_dim ** (-0.5)
    half = 128
    per = half // head_dim
    hid = lax.broadcasted_iota(jnp.int32, (per, 1, half), 0)
    lid = lax.broadcasted_iota(jnp.int32, (per, 1, half), 2) // head_dim
    hm32 = jnp.where(hid == lid, 1.0, 0.0).astype(F32)
    hm = hm32.astype(BF16)
    kid = lax.broadcasted_iota(jnp.int32, (cells, cells), 0)
    qid = lax.broadcasted_iota(jnp.int32, (cells, cells), 1)
    mid = WIN * SHIFT
    row_diff = jnp.where((kid >= mid) != (qid >= mid), MASKED_SCORE, 0.0)
    kcol, qcol = lax.rem(kid, WIN) >= SHIFT, lax.rem(qid, WIN) >= SHIFT
    col_diff = jnp.where(kcol != qcol, MASKED_SCORE, 0.0)
    row_bias = row_diff * jnp.where(me_r == rows - 1, 1.0, 0.0)
    last_col = me_c == cols - 1

    def window(w):
        edge = jnp.where(jnp.logical_and(last_col, w == windows - 1), 1.0, 0.0)
        bias = (row_bias + col_diff * edge)[None]
        for t in range(channels // half):
            at = slice(t * half, (t + 1) * half)
            k_at = slice(channels + t * half, channels + (t + 1) * half)
            v_at = slice(2 * channels + t * half, 2 * channels + (t + 1) * half)
            q = proj[w, :, at]
            k = proj[w, :, k_at]
            v = proj[w, :, v_at]
            dc = dctx[w, :, at]
            kx = (k[None] * hm).reshape(per * cells, half)
            vx = (v[None] * hm).reshape(per * cells, half)
            s = nt(kx, q).reshape(per, cells, cells) + bias
            peak = jnp.max(s, 1, keepdims=True)
            e = jnp.exp2((s - peak) * (scale * LOG2E))
            p = e * (1.0 / jnp.sum(e, 1, keepdims=True))
            pb = p.astype(BF16).reshape(per * cells, cells)
            ctx[w, :, at] = tn(pb, vx).astype(BF16)
            dp = nt(vx, dc).astype(BF16).astype(F32).reshape(per, cells, cells)
            ds = p * (dp - jnp.sum(p * dp, 1, keepdims=True))
            dsb = ds.astype(BF16).reshape(per * cells, cells)
            dproj[w, :, at] = (tn(dsb, kx) * scale).astype(BF16)
            dk = nn(dsb, q).reshape(per, cells, half) * hm32
            dproj[w, :, k_at] = (jnp.sum(dk, 0) * scale).astype(BF16)
            dv = nn(pb, dc).reshape(per, cells, half) * hm32
            dproj[w, :, v_at] = jnp.sum(dv, 0).astype(BF16)

    def step(i, carry):
        window(2 * i)
        window(2 * i + 1)
        return carry

    lax.fori_loop(0, windows // 2, step, 0)

    flat_p = dproj[...].reshape(total, 3 * channels)
    flat_c = ctx[...].reshape(total, channels)
    hrows = channels // 2
    part[:, :, 0 : 3 * channels] = tn(flat_s, flat_p).reshape(2, hrows, 3 * channels)
    part[:, :, 3 * channels :] = tn(flat_c, flat_d).reshape(2, hrows, channels)
    other = dev(me_r, c_right)
    core_out[...] = part[c_right].astype(BF16)
    core_copy = remote(core_out, core_in, core_send.at[0], core_recv.at[0], other)
    core_copy.start()

    dnormed = nt(flat_p, wqkv_ref[...]).astype(BF16).astype(F32)
    attended = nn(flat_c, wproj_ref[...]).astype(BF16).astype(F32)
    gsum = jnp.zeros((WIN, channels), F32)
    for w in range(windows):
        at = slice(w * WIN + SHIFT, (w + 1) * WIN + SHIFT)
        dn = dnormed[w * cells : (w + 1) * cells]
        standard = xhat[w]
        gsum = gsum + jnp.sum((dn * standard).reshape(WIN, WIN, channels), 0)
        up_grad = dn * gain
        mean_g = jnp.mean(up_grad, -1, keepdims=True)
        mean_gx = jnp.mean(up_grad * standard, -1, keepdims=True)
        grad = rstd[w] * (up_grad - mean_g - standard * mean_gx)
        out32[1, :, at, :] = cf[:, at, :] + grad.reshape(WIN, WIN, channels)
        inside = mask[w] * attended[w * cells : (w + 1) * cells]
        out32[0, :, at, :] = xf[:, at, :] + inside.reshape(WIN, WIN, channels)
    gtile = jnp.concatenate([gsum[:, :half], gsum[:, half:]], 0)
    gcore_out[...] = gtile.astype(BF16)
    gain_copy = remote(gcore_out, gcore_in, core_send.at[1], core_recv.at[1], other)
    gain_copy.start()
    outx[...] = out32[...].astype(BF16)
    both = pl.ds(0, 2)
    outs = [
        remote(
            outx.at[both, low, body], row_in, out_send.at[0], out_recv.at[0], dev(r_dn, me_c)
        ),
        remote(
            outx.at[both, top, side], col_in, out_send.at[1], out_recv.at[1], dev(me_r, c_right)
        ),
        remote(
            outx.at[both, low, side], diag_in, out_send.at[2], out_recv.at[2], dev(r_dn, c_right)
        ),
    ]

    wide = 4 * channels
    core_copy.wait()
    gain_copy.wait()
    gchip = (gtile + gcore_in[...].astype(F32)).astype(BF16)
    chip = (part[me_c] + core_in[...].astype(F32)).astype(BF16)
    sbuf[:, :, 0:wide] = chip.reshape(INNER, hrows // INNER, wide)
    for j in range(INNER):
        sbuf[j, :, wide:] = gchip
    scatter = [
        remote(
            sbuf.at[lax.rem(member + o, INNER)],
            rbuf.at[o],
            rs_send.at[o],
            rs_recv.at[o],
            dev(peer(o), me_c),
        )
        for o in range(1, INNER)
    ]
    for copy in scatter:
        copy.start()
    for copy in outs:
        copy.start()
    acc = sbuf[member].astype(F32)
    for o in range(1, INNER):
        scatter[o - 1].wait()
        acc = acc + rbuf[o].astype(F32)
    if outer > 1:
        obuf[...] = acc.astype(BF16)
        spread = [
            remote(obuf, oin.at[o], o_send.at[o], o_recv.at[o], dev(counterpart(o), me_c))
            for o in range(1, outer)
        ]
        for copy in spread:
            copy.start()
        for o in range(1, outer):
            spread[o - 1].wait()
            acc = acc + oin[o].astype(F32)

    mine = gsum_ref.at[me_c, member]
    mine[...] = acc[:, 0:wide].astype(BF16)
    gather = [
        remote(mine, mine, ag_send.at[o], ag_recv.at[o], dev(peer(o), me_c))
        for o in range(1, INNER)
    ]
    for copy in gather:
        copy.start()
    forward = [remote(mine, mine, fw_send.at[0], fw_recv.at[0], other)]
    forward[0].start()
    gfold = jnp.concatenate([acc[0:WIN, wide:], acc[WIN:, wide:]], 1)
    ggain_ref[...] = jnp.sum(gfold, 0, keepdims=True)

    for copy in outs:
        copy.wait()
    col_id = lax.broadcasted_iota(jnp.int32, (SHIFT, PAD, channels), 1)
    for n, ref in enumerate((upd_ref, gfeat_ref)):
        ref[0:SHIFT, PAD:, :] = row_in[n, :, PAD:, :]
        ref[SHIFT:, PAD:, :] = outx[n, 0:SHIFT, PAD:tile_cols, :]
        ref[0:SHIFT, 0:PAD, :] = jnp.where(
            col_id < SHIFT, diag_in[n].astype(F32), row_in[n, :, 0:PAD, :].astype(F32)
        ).astype(BF16)
        ref[SHIFT:, 0:PAD, :] = jnp.where(
            col_id < SHIFT, col_in[n].astype(F32), outx[n, 0:SHIFT, 0:PAD, :].astype(F32)
        ).astype(BF16)

    for o in range(1, INNER):
        gather[o - 1].wait()
        piece = gsum_ref.at[me_c, lax.rem(member + INNER - o, INNER)]
        copy = remote(piece, piece, fw_send.at[o], fw_recv.at[o], other)
        copy.start()
        forward.append(copy)
    for copy in forward:
        copy.wait()


def on_device(features, cotangent, domain, qkv_weight, proj_weight, norm_gain):
    tile_rows, tile_cols, channels = features.shape
    rows, cols = lax.axis_size("row"), lax.axis_size("col")
    outer = rows // INNER
    windows, cells = tile_cols // WIN, WIN * WIN
    piece = channels // 2 // INNER
    wide = 4 * channels
    ext = tile_cols + PAD
    vm = pltpu.VMEM
    dma = pltpu.SemaphoreType.DMA
    dom = domain.astype(F32)
    dom = jnp.concatenate([dom, dom], 1)
    vspec = pl.BlockSpec(memory_space=pltpu.VMEM)
    updated, grad_features, gsum, ggain = pl.pallas_call(
        functools.partial(kernel, rows, cols),
        out_shape=(
            jax.ShapeDtypeStruct(features.shape, BF16),
            jax.ShapeDtypeStruct(features.shape, BF16),
            jax.ShapeDtypeStruct((2, INNER, piece, wide), BF16),
            jax.ShapeDtypeStruct((1, channels), F32),
        ),
        in_specs=[vspec] * 6,
        out_specs=(vspec,) * 4,
        scratch_shapes=[
            vm((tile_rows, ext, channels), BF16),
            vm((tile_rows, ext, channels), BF16),
            vm((3, tile_rows, 2 * tile_cols), F32),
            vm((tile_rows, ext, channels), F32),
            vm((tile_rows, ext, channels), F32),
            vm((tile_rows, 2 * tile_cols), F32),
            vm((windows, cells, 1), F32),
            vm((windows, cells, channels), F32),
            vm((windows, cells, 1), F32),
            vm((windows, cells, channels), BF16),
            vm((windows, cells, channels), BF16),
            vm((windows, cells, 3 * channels), BF16),
            vm((windows, cells, 3 * channels), BF16),
            vm((windows, cells, channels), BF16),
            vm((windows, cells, channels), BF16),
            vm((2, tile_rows, ext, channels), F32),
            vm((2, tile_rows, ext, channels), BF16),
            vm((2, SHIFT, tile_cols, channels), BF16),
            vm((2, SHIFT, PAD, channels), BF16),
            vm((2, SHIFT, PAD, channels), BF16),
            vm((2, channels // 2, wide), F32),
            vm((channels // 2, wide), BF16),
            vm((channels // 2, wide), BF16),
            vm((16, 128), BF16),
            vm((16, 128), BF16),
            vm((INNER, piece, wide + 128), BF16),
            vm((INNER, piece, wide + 128), BF16),
            vm((piece, wide + 128), BF16),
            vm((outer, piece, wide + 128), BF16),
            dma((9,)),
            dma((9,)),
            dma((3,)),
            dma((3,)),
            dma((2,)),
            dma((2,)),
            dma((INNER,)),
            dma((INNER,)),
            dma((outer,)),
            dma((outer,)),
            dma((INNER,)),
            dma((INNER,)),
            dma((INNER,)),
            dma((INNER,)),
        ],
        compiler_params=pltpu.CompilerParams(
            collective_id=0, has_side_effects=True, vmem_limit_bytes=48 * 1024 * 1024
        ),
    )(features, cotangent, dom, qkv_weight, proj_weight, norm_gain[None, :])
    sums = gsum.reshape(channels, wide).astype(F32)
    return (
        updated,
        grad_features,
        sums[:, : 3 * channels],
        sums[:, 3 * channels :],
        ggain.reshape(channels),
    )


def solution(mesh):
    return jax.shard_map(
        on_device,
        mesh=mesh,
        in_specs=(
            P(("grp", "row"), "col", None),
            P(("grp", "row"), "col", None),
            P(("grp", "row"), "col"),
            P(),
            P(),
            P(),
        ),
        out_specs=(
            P(("grp", "row"), "col", None),
            P(("grp", "row"), "col", None),
            P("grp", None),
            P("grp", None),
            P("grp"),
        ),
        check_vma=False,
    )
```

```python
import functools

import jax
import jax.numpy as jnp
from jax import lax
from jax.experimental import pallas as pl
from jax.experimental.pallas import tpu as pltpu
from jax.sharding import PartitionSpec as P

HEADS = 8
WIN = 8
SHIFT = 4
NORM_EPSILON = 1e-05
MASKED_SCORE = -1e30
LOG2E = 1.4426950408889634
INNER = 8
PAD = 16

F32 = jnp.float32
BF16 = jnp.bfloat16


def nn(a, b):
    return lax.dot_general(a, b, (((1,), (0,)), ((), ())), preferred_element_type=F32)


def nt(a, b):
    return lax.dot_general(a, b, (((1,), (1,)), ((), ())), preferred_element_type=F32)


def tn(a, b):
    return lax.dot_general(a, b, (((0,), (0,)), ((), ())), preferred_element_type=F32)


def kernel(
    rows,
    cols,
    feat_hbm,
    cot_hbm,
    dom_hbm,
    wqkv_hbm,
    wproj_hbm,
    gain_hbm,
    upd_hbm,
    gfeat_hbm,
    gsum_hbm,
    ggain_hbm,
    upd_ref,
    gfeat_ref,
    gsum_ref,
    ggain_ref,
    wqkv_ref,
    wproj_ref,
    gain_ref,
    dom_ref,
    dom_out,
    ext_f,
    ext_c,
    ext_d,
    xf,
    cf,
    dx,
    mask,
    xhat,
    rstd,
    shifted,
    datt,
    proj,
    dproj,
    ctx,
    dctx,
    out32,
    outx,
    row_in,
    col_in,
    diag_in,
    own_part,
    core_out,
    core_in,
    gcore_out,
    gcore_in,
    sbuf,
    rbuf,
    obuf,
    oin,
    local_sem,
    done_sem,
    in_send,
    in_recv,
    out_send,
    out_recv,
    core_send,
    core_recv,
    rs_send,
    rs_recv,
    o_send,
    o_recv,
    ag_send,
    ag_recv,
    fw_send,
    fw_recv,
):
    tile_rows, tile_cols, channels = feat_hbm.shape
    windows = tile_cols // WIN
    cells = WIN * WIN
    head_dim = channels // HEADS
    blocks = tile_cols // PAD
    each = PAD // WIN
    outer = rows // INNER
    me_r = lax.axis_index("row")
    me_c = lax.axis_index("col")
    r_up = lax.rem(me_r + rows - 1, rows)
    r_dn = lax.rem(me_r + 1, rows)
    c_left = lax.rem(me_c + cols - 1, cols)
    c_right = lax.rem(me_c + 1, cols)
    group = me_r // INNER
    member = lax.rem(me_r, INNER)

    def dev(r, c):
        return {"row": r, "col": c}

    def peer(o):
        return group * INNER + lax.rem(member + o, INNER)

    def counterpart(o):
        return lax.rem(group + o, outer) * INNER + member

    barrier = pltpu.get_barrier_semaphore()
    greeted = [
        dev(r_up, me_c),
        dev(r_dn, me_c),
        dev(me_r, c_left),
        dev(r_up, c_left),
        dev(r_dn, c_right),
    ]
    greeted += [dev(peer(o), me_c) for o in range(1, INNER)]
    greeted += [dev(counterpart(o), me_c) for o in range(1, outer)]
    for target in greeted:
        pl.semaphore_signal(barrier, inc=1, device_id=target, device_id_type=pl.DeviceIdType.MESH)

    top, low = pl.ds(0, SHIFT), pl.ds(SHIFT, SHIFT)
    body, side, head = pl.ds(0, tile_cols), pl.ds(tile_cols, PAD), pl.ds(0, PAD)
    local = [
        pltpu.make_async_copy(s, d, local_sem.at[i])
        for i, (s, d) in enumerate(
            (
                (dom_hbm, dom_ref),
                (feat_hbm.at[low], ext_f.at[top, body]),
                (cot_hbm.at[low], ext_c.at[top, body]),
                (gain_hbm, gain_ref),
                (wqkv_hbm, wqkv_ref),
                (wproj_hbm, wproj_ref),
            )
        )
    ]
    for copy in local:
        copy.start()
    out32[:, :, 0:8, :] = jnp.zeros((2, tile_rows, 8, channels), F32)
    out32[:, :, tile_cols : tile_cols + PAD, :] = jnp.zeros((2, tile_rows, PAD, channels), F32)
    local[0].wait()
    dom = dom_ref[...].astype(F32)
    dom_out[...] = jnp.concatenate([dom, dom], 1)
    pl.semaphore_wait(barrier, len(greeted))

    def remote(src, dst, send, recv, target):
        return pltpu.make_async_remote_copy(
            src_ref=src,
            dst_ref=dst,
            send_sem=send,
            recv_sem=recv,
            device_id=target,
            device_id_type=pl.DeviceIdType.MESH,
        )

    up, left, corner = dev(r_up, me_c), dev(me_r, c_left), dev(r_up, c_left)
    pairs = ((feat_hbm, ext_f), (cot_hbm, ext_c))
    jobs = [(dom_out, ext_d.at[i], t) for i, t in enumerate((up, left, corner))]
    for b in range(blocks):
        block = pl.ds(b * PAD, PAD)
        jobs += [(s.at[top, block], d.at[low, block], up) for s, d in pairs]
    jobs += [(s.at[low, head], d.at[top, side], left) for s, d in pairs]
    jobs += [(s.at[top, head], d.at[low, side], corner) for s, d in pairs]
    halos = [
        remote(s, d, in_send.at[i], in_recv.at[i], t) for i, (s, d, t) in enumerate(jobs)
    ]
    for copy in halos:
        copy.start()
    for copy in local[1:]:
        copy.wait()
    gain = gain_ref[...]

    scale = head_dim ** (-0.5)
    half = 128
    per = half // head_dim
    hid = lax.broadcasted_iota(jnp.int32, (per, 1, half), 0)
    lid = lax.broadcasted_iota(jnp.int32, (per, 1, half), 2) // head_dim
    hm32 = jnp.where(hid == lid, 1.0, 0.0).astype(F32)
    hm = hm32.astype(BF16)
    kid = lax.broadcasted_iota(jnp.int32, (cells, cells), 0)
    qid = lax.broadcasted_iota(jnp.int32, (cells, cells), 1)
    mid = WIN * SHIFT
    row_diff = jnp.where((kid >= mid) != (qid >= mid), MASKED_SCORE, 0.0)
    kcol, qcol = lax.rem(kid, WIN) >= SHIFT, lax.rem(qid, WIN) >= SHIFT
    col_diff = jnp.where(kcol != qcol, MASKED_SCORE, 0.0)
    row_bias = row_diff * jnp.where(me_r == rows - 1, 1.0, 0.0)
    last_bias = row_bias + col_diff * jnp.where(me_c == cols - 1, 1.0, 0.0)

    for copy in halos[0:3]:
        copy.wait()
    lane = lax.broadcasted_iota(jnp.int32, (SHIFT, 2 * tile_cols), 1)
    dx[0:SHIFT, :] = jnp.where(lane < tile_cols, dom_out[SHIFT:, :], ext_d[1, SHIFT:, :])
    dx[SHIFT:, :] = jnp.where(lane < tile_cols, ext_d[0, 0:SHIFT, :], ext_d[2, 0:SHIFT, :])
    pick = lax.broadcasted_iota(jnp.int32, (WIN, 2 * tile_cols), 1) - lax.broadcasted_iota(
        jnp.int32, (WIN, 2 * tile_cols), 0
    )

    def attend(w):
        bias = (last_bias if w == windows - 1 else row_bias)[None]
        for t in range(channels // half):
            at = slice(t * half, (t + 1) * half)
            k_at = slice(channels + t * half, channels + (t + 1) * half)
            v_at = slice(2 * channels + t * half, 2 * channels + (t + 1) * half)
            q = proj[w, :, at]
            k = proj[w, :, k_at]
            v = proj[w, :, v_at]
            dc = dctx[w, :, at]
            kx = (k[None] * hm).reshape(per * cells, half)
            vx = (v[None] * hm).reshape(per * cells, half)
            s = nt(kx, q).reshape(per, cells, cells) + bias
            peak = jnp.max(s, 1, keepdims=True)
            e = jnp.exp2((s - peak) * (scale * LOG2E))
            p = e * (1.0 / jnp.sum(e, 1, keepdims=True))
            pb = p.astype(BF16).reshape(per * cells, cells)
            ctx[w, :, at] = tn(pb, vx).astype(BF16)
            dp = nt(vx, dc).astype(BF16).astype(F32).reshape(per, cells, cells)
            ds = p * (dp - jnp.sum(p * dp, 1, keepdims=True))
            dsb = ds.astype(BF16).reshape(per * cells, cells)
            dproj[w, :, at] = (tn(dsb, kx) * scale).astype(BF16)
            dk = nn(dsb, q).reshape(per, cells, half) * hm32
            dproj[w, :, k_at] = (jnp.sum(dk, 0) * scale).astype(BF16)
            dv = nn(pb, dc).reshape(per, cells, half) * hm32
            dproj[w, :, v_at] = jnp.sum(dv, 0).astype(BF16)

    gsum = jnp.zeros((WIN, channels), F32)
    both = pl.ds(0, 2)
    outs = []
    for b in range(blocks):
        for n in (0, 1) if b == 0 else (b + 1,):
            first = 3 + 2 * n
            for copy in halos[first : first + (2 if n < blocks else 4)]:
                copy.wait()
            block = slice(n * PAD, (n + 1) * PAD)
            xf[:, block, :] = ext_f[:, block, :].astype(F32)
            cf[:, block, :] = ext_c[:, block, :].astype(F32)
        mine_w = range(b * each, (b + 1) * each)
        for w in mine_w:
            for i in range(tile_rows):
                line = jnp.broadcast_to(dx[i : i + 1, :], (WIN, 2 * tile_cols))
                mask[w, i * WIN : (i + 1) * WIN, :] = jnp.sum(
                    jnp.where(pick == w * WIN + SHIFT, line, 0.0), -1, keepdims=True
                )
            at = slice(w * WIN + SHIFT, (w + 1) * WIN + SHIFT)
            x = xf[:, at, :].reshape(cells, channels)
            average = jnp.mean(x, -1, keepdims=True)
            centred = x - average
            variance = jnp.mean(centred * centred, -1, keepdims=True)
            inv = lax.rsqrt(variance + NORM_EPSILON)
            standard = centred * inv
            rstd[w] = inv
            xhat[w] = standard
            shifted[w] = (standard * gain).astype(BF16)
            c = cf[:, at, :].reshape(cells, channels)
            datt[w] = (c * mask[w]).astype(BF16)
        ws = slice(b * each, (b + 1) * each)
        count = each * cells
        s_chunk = shifted[ws].reshape(count, channels)
        d_chunk = datt[ws].reshape(count, channels)
        proj[ws] = nn(s_chunk, wqkv_ref[...]).astype(BF16).reshape(each, cells, 3 * channels)
        dctx[ws] = nt(d_chunk, wproj_ref[...]).astype(BF16).reshape(each, cells, channels)
        for w in mine_w:
            attend(w)
        p_chunk = dproj[ws].reshape(count, 3 * channels)
        dnormed = nt(p_chunk, wqkv_ref[...]).astype(BF16).astype(F32)
        c_chunk = ctx[ws].reshape(count, channels)
        attended = nn(c_chunk, wproj_ref[...]).astype(BF16).astype(F32)
        for u, w in enumerate(mine_w):
            at = slice(w * WIN + SHIFT, (w + 1) * WIN + SHIFT)
            dn = dnormed[u * cells : (u + 1) * cells]
            standard = xhat[w]
            gsum = gsum + jnp.sum((dn * standard).reshape(WIN, WIN, channels), 0)
            up_grad = dn * gain
            mean_g = jnp.mean(up_grad, -1, keepdims=True)
            mean_gx = jnp.mean(up_grad * standard, -1, keepdims=True)
            grad = rstd[w] * (up_grad - mean_g - standard * mean_gx)
            out32[1, :, at, :] = cf[:, at, :] + grad.reshape(WIN, WIN, channels)
            inside = mask[w] * attended[u * cells : (u + 1) * cells]
            out32[0, :, at, :] = xf[:, at, :] + inside.reshape(WIN, WIN, channels)
        block = slice(b * PAD, (b + 1) * PAD)
        outx[:, :, block, :] = out32[:, :, block, :].astype(BF16)
        area = pl.ds(b * PAD, PAD)
        copy = remote(
            outx.at[both, low, area],
            row_in.at[both, top, area],
            out_send.at[b],
            out_recv.at[b],
            dev(r_dn, me_c),
        )
        copy.start()
        outs.append(copy)

    total = windows * cells
    hrows = channels // 2
    wide = 4 * channels
    other = dev(me_r, c_right)
    flat_p = dproj[...].reshape(total, 3 * channels)
    flat_d = datt[...].reshape(total, channels)

    def half_sum(core):
        at = pl.ds(pl.multiple_of(core * hrows, hrows), hrows)
        left_s = shifted[:, :, at].reshape(total, hrows)
        left_c = ctx[:, :, at].reshape(total, hrows)
        return tn(left_s, flat_p), tn(left_c, flat_d)

    sum_q, sum_p = half_sum(c_right)
    core_out[:, 0 : 3 * channels] = sum_q.astype(BF16)
    core_out[:, 3 * channels :] = sum_p.astype(BF16)
    core_copy = remote(core_out, core_in, core_send.at[0], core_recv.at[0], other)
    core_copy.start()
    gtile = jnp.concatenate([gsum[:, :half], gsum[:, half:]], 0)
    gcore_out[...] = gtile.astype(BF16)
    gain_copy = remote(gcore_out, gcore_in, core_send.at[1], core_recv.at[1], other)
    gain_copy.start()
    sum_q, sum_p = half_sum(me_c)
    own_part[:, 0 : 3 * channels] = sum_q
    own_part[:, 3 * channels :] = sum_p
    edge = slice(tile_cols, tile_cols + PAD)
    outx[:, :, edge, :] = out32[:, :, edge, :].astype(BF16)

    core_copy.wait()
    gain_copy.wait()
    gchip = (gtile + gcore_in[...].astype(F32)).astype(BF16)
    share = hrows // INNER

    def chip_sum(j):
        at = pl.ds(pl.multiple_of(j * share, share), share)
        sbuf[j, :, 0:wide] = (own_part[at, :] + core_in[at, :].astype(F32)).astype(BF16)
        sbuf[j, :, wide:] = gchip

    scatter = [None]
    for o in range(1, INNER):
        j = lax.rem(member + o, INNER)
        chip_sum(j)
        copy = remote(sbuf.at[j], rbuf.at[o], rs_send.at[o], rs_recv.at[o], dev(peer(o), me_c))
        copy.start()
        scatter.append(copy)
    last = [
        remote(
            outx.at[both, top, side],
            col_in,
            out_send.at[blocks],
            out_recv.at[blocks],
            dev(me_r, c_right),
        ),
        remote(
            outx.at[both, low, side],
            diag_in,
            out_send.at[blocks + 1],
            out_recv.at[blocks + 1],
            dev(r_dn, c_right),
        ),
    ]
    for copy in last:
        copy.start()
    outs += last
    chip_sum(member)
    acc = sbuf[member].astype(F32)
    for o in range(1, INNER):
        scatter[o].wait()
        acc = acc + rbuf[o].astype(F32)
    if outer > 1:
        obuf[...] = acc.astype(BF16)
        spread = [
            remote(obuf, oin.at[o], o_send.at[o], o_recv.at[o], dev(counterpart(o), me_c))
            for o in range(1, outer)
        ]
        for copy in spread:
            copy.start()
        for o in range(1, outer):
            spread[o - 1].wait()
            acc = acc + oin[o].astype(F32)

    mine = gsum_ref.at[me_c, member]
    mine[...] = acc[:, 0:wide].astype(BF16)
    gather = [
        remote(mine, mine, ag_send.at[o], ag_recv.at[o], dev(peer(o), me_c))
        for o in range(1, INNER)
    ]
    for copy in gather:
        copy.start()
    forward = [remote(mine, mine, fw_send.at[0], fw_recv.at[0], other)]
    forward[0].start()
    gfold = jnp.concatenate([acc[0:WIN, wide:], acc[WIN:, wide:]], 1)
    ggain_ref[...] = jnp.sum(gfold, 0, keepdims=True)

    def give(i, src, dst):
        copy = pltpu.make_async_copy(src, dst, done_sem.at[i])
        copy.start()
        return copy

    results = [give(0, ggain_ref, ggain_hbm)]
    for copy in outs:
        copy.wait()
    col_id = lax.broadcasted_iota(jnp.int32, (SHIFT, PAD, channels), 1)
    for n, ref in enumerate((upd_ref, gfeat_ref)):
        ref[0:SHIFT, PAD:, :] = row_in[n, :, PAD:, :]
        ref[SHIFT:, PAD:, :] = outx[n, 0:SHIFT, PAD:tile_cols, :]
        ref[0:SHIFT, 0:PAD, :] = jnp.where(
            col_id < SHIFT, diag_in[n].astype(F32), row_in[n, :, 0:PAD, :].astype(F32)
        ).astype(BF16)
        ref[SHIFT:, 0:PAD, :] = jnp.where(
            col_id < SHIFT, col_in[n].astype(F32), outx[n, 0:SHIFT, 0:PAD, :].astype(F32)
        ).astype(BF16)
    results += [give(1, upd_ref, upd_hbm), give(2, gfeat_ref, gfeat_hbm)]

    for o in range(1, INNER):
        gather[o - 1].wait()
        piece = gsum_ref.at[me_c, lax.rem(member + INNER - o, INNER)]
        copy = remote(piece, piece, fw_send.at[o], fw_recv.at[o], other)
        copy.start()
        forward.append(copy)
    results.append(give(3, gsum_ref.at[me_c], gsum_hbm.at[me_c]))
    for copy in forward:
        copy.wait()
    results.append(give(4, gsum_ref.at[c_right], gsum_hbm.at[c_right]))
    for copy in results:
        copy.wait()


def finish(
    upd_in, gfeat_in, gsum_in, ggain_in, upd, gfeat, gqkv, gproj, ggain, sums, qkv32, proj32, sems
):
    channels = gqkv.shape[0]
    halves, _, _, wide = sums.shape
    hrows = channels // halves
    jobs = [(gsum_in.at[c], sums.at[c]) for c in range(halves)]
    jobs += [(upd_in, upd), (gfeat_in, gfeat), (ggain_in, ggain)]
    first = len(jobs)
    for c in range(halves):
        at = pl.ds(c * hrows, hrows)
        jobs += [(proj32.at[at], gproj.at[at]), (qkv32.at[at], gqkv.at[at])]
    copies = [pltpu.make_async_copy(s, d, sems.at[i]) for i, (s, d) in enumerate(jobs)]
    for copy in copies[0:first]:
        copy.start()
    for c in range(halves):
        copies[c].wait()
        at = slice(c * hrows, (c + 1) * hrows)
        some = sums[c].reshape(hrows, wide)
        proj32[at, :] = some[:, 3 * channels :].astype(F32)
        copies[first + 2 * c].start()
        qkv32[at, :] = some[:, : 3 * channels].astype(F32)
        copies[first + 2 * c + 1].start()
    for copy in copies[halves:]:
        copy.wait()


def on_device(features, cotangent, domain, qkv_weight, proj_weight, norm_gain):
    tile_rows, tile_cols, channels = features.shape
    rows, cols = lax.axis_size("row"), lax.axis_size("col")
    outer = rows // INNER
    windows, cells = tile_cols // WIN, WIN * WIN
    blocks = tile_cols // PAD
    piece = channels // 2 // INNER
    wide = 4 * channels
    ext = tile_cols + PAD
    vm = pltpu.VMEM
    dma = pltpu.SemaphoreType.DMA
    halos = 3 + 2 * blocks + 4
    aspec = pl.BlockSpec(memory_space=pltpu.HBM)
    results = pl.pallas_call(
        functools.partial(kernel, rows, cols),
        out_shape=(
            jax.ShapeDtypeStruct(features.shape, BF16),
            jax.ShapeDtypeStruct(features.shape, BF16),
            jax.ShapeDtypeStruct((2, INNER, piece, wide), BF16),
            jax.ShapeDtypeStruct((1, channels), F32),
        ),
        in_specs=[aspec] * 6,
        out_specs=(aspec,) * 4,
        scratch_shapes=[
            vm(features.shape, BF16),
            vm(features.shape, BF16),
            vm((2, INNER, piece, wide), BF16),
            vm((1, channels), F32),
            vm(qkv_weight.shape, BF16),
            vm(proj_weight.shape, BF16),
            vm((1, channels), F32),
            vm((tile_rows, tile_cols), jnp.int32),
            vm((tile_rows, 2 * tile_cols), F32),
            vm((tile_rows, ext, channels), BF16),
            vm((tile_rows, ext, channels), BF16),
            vm((3, tile_rows, 2 * tile_cols), F32),
            vm((tile_rows, ext, channels), F32),
            vm((tile_rows, ext, channels), F32),
            vm((tile_rows, 2 * tile_cols), F32),
            vm((windows, cells, 1), F32),
            vm((windows, cells, channels), F32),
            vm((windows, cells, 1), F32),
            vm((windows, cells, channels), BF16),
            vm((windows, cells, channels), BF16),
            vm((windows, cells, 3 * channels), BF16),
            vm((windows, cells, 3 * channels), BF16),
            vm((windows, cells, channels), BF16),
            vm((windows, cells, channels), BF16),
            vm((2, tile_rows, ext, channels), F32),
            vm((2, tile_rows, ext, channels), BF16),
            vm((2, SHIFT, tile_cols, channels), BF16),
            vm((2, SHIFT, PAD, channels), BF16),
            vm((2, SHIFT, PAD, channels), BF16),
            vm((channels // 2, wide), F32),
            vm((channels // 2, wide), BF16),
            vm((channels // 2, wide), BF16),
            vm((16, 128), BF16),
            vm((16, 128), BF16),
            vm((INNER, piece, wide + 128), BF16),
            vm((INNER, piece, wide + 128), BF16),
            vm((piece, wide + 128), BF16),
            vm((outer, piece, wide + 128), BF16),
            dma((6,)),
            dma((5,)),
            dma((halos,)),
            dma((halos,)),
            dma((blocks + 2,)),
            dma((blocks + 2,)),
            dma((2,)),
            dma((2,)),
            dma((INNER,)),
            dma((INNER,)),
            dma((outer,)),
            dma((outer,)),
            dma((INNER,)),
            dma((INNER,)),
            dma((INNER,)),
            dma((INNER,)),
        ],
        compiler_params=pltpu.CompilerParams(
            collective_id=0, has_side_effects=True, vmem_limit_bytes=60 * 1024 * 1024
        ),
    )(features, cotangent, domain, qkv_weight, proj_weight, norm_gain[None, :])
    outs = pl.pallas_call(
        finish,
        out_shape=(
            jax.ShapeDtypeStruct(features.shape, BF16),
            jax.ShapeDtypeStruct(features.shape, BF16),
            jax.ShapeDtypeStruct((channels, 3 * channels), F32),
            jax.ShapeDtypeStruct((channels, channels), F32),
            jax.ShapeDtypeStruct((1, channels), F32),
        ),
        in_specs=[aspec] * 4,
        out_specs=(aspec,) * 5,
        scratch_shapes=[
            vm((2, INNER, piece, wide), BF16),
            vm((channels, 3 * channels), F32),
            vm((channels, channels), F32),
            dma((9,)),
        ],
        compiler_params=pltpu.CompilerParams(vmem_limit_bytes=60 * 1024 * 1024),
    )(*results)
    return (outs[0], outs[1], outs[2], outs[3], outs[4].reshape(channels))


def solution(mesh):
    return jax.shard_map(
        on_device,
        mesh=mesh,
        in_specs=(
            P(("grp", "row"), "col", None),
            P(("grp", "row"), "col", None),
            P(("grp", "row"), "col"),
            P(),
            P(),
            P(),
        ),
        out_specs=(
            P(("grp", "row"), "col", None),
            P(("grp", "row"), "col", None),
            P("grp", None),
            P("grp", None),
            P("grp"),
        ),
        check_vma=False,
    )
```

```python
import functools

import jax
import jax.numpy as jnp
from jax import lax
from jax.experimental import pallas as pl
from jax.experimental.pallas import tpu as pltpu
from jax.sharding import PartitionSpec as P

HEADS = 8
WIN = 8
SHIFT = 4
NORM_EPSILON = 1e-05
MASKED_SCORE = -1e30
LOG2E = 1.4426950408889634
INNER = 8
PAD = 16

F32 = jnp.float32
BF16 = jnp.bfloat16


def nn(a, b):
    return lax.dot_general(a, b, (((1,), (0,)), ((), ())), preferred_element_type=F32)


def nt(a, b):
    return lax.dot_general(a, b, (((1,), (1,)), ((), ())), preferred_element_type=F32)


def tn(a, b):
    return lax.dot_general(a, b, (((0,), (0,)), ((), ())), preferred_element_type=F32)


def kernel(
    rows,
    cols,
    feat_hbm,
    cot_hbm,
    dom_hbm,
    wqkv_hbm,
    wproj_hbm,
    gain_hbm,
    upd_hbm,
    gfeat_hbm,
    gsum_hbm,
    ggain_hbm,
    upd_ref,
    gfeat_ref,
    gsum_ref,
    ggain_ref,
    wqkv_ref,
    wproj_ref,
    gain_ref,
    dom_ref,
    dom_out,
    ext_f,
    ext_c,
    ext_d,
    xf,
    cf,
    dx,
    mask,
    xhat,
    rstd,
    shifted,
    datt,
    proj,
    dproj,
    ctx,
    dctx,
    out32,
    outx,
    row_in,
    col_in,
    diag_in,
    own_part,
    core_out,
    core_in,
    gcore_out,
    gcore_in,
    sbuf,
    rbuf,
    obuf,
    oin,
    local_sem,
    done_sem,
    in_send,
    in_recv,
    out_send,
    out_recv,
    core_send,
    core_recv,
    rs_send,
    rs_recv,
    o_send,
    o_recv,
    ag_send,
    ag_recv,
    fw_send,
    fw_recv,
):
    tile_rows, tile_cols, channels = feat_hbm.shape
    windows = tile_cols // WIN
    cells = WIN * WIN
    head_dim = channels // HEADS
    blocks = tile_cols // PAD
    each = PAD // WIN
    outer = rows // INNER
    me_r = lax.axis_index("row")
    me_c = lax.axis_index("col")
    r_up = lax.rem(me_r + rows - 1, rows)
    r_dn = lax.rem(me_r + 1, rows)
    c_left = lax.rem(me_c + cols - 1, cols)
    c_right = lax.rem(me_c + 1, cols)
    group = me_r // INNER
    member = lax.rem(me_r, INNER)

    def dev(r, c):
        return {"row": r, "col": c}

    def peer(o):
        return group * INNER + lax.rem(member + o, INNER)

    def counterpart(o):
        return lax.rem(group + o, outer) * INNER + member

    barrier = pltpu.get_barrier_semaphore()
    greeted = [
        dev(r_up, me_c),
        dev(r_dn, me_c),
        dev(me_r, c_left),
        dev(r_up, c_left),
        dev(r_dn, c_right),
    ]
    greeted += [dev(peer(o), me_c) for o in range(1, INNER)]
    greeted += [dev(counterpart(o), me_c) for o in range(1, outer)]
    for target in greeted:
        pl.semaphore_signal(barrier, inc=1, device_id=target, device_id_type=pl.DeviceIdType.MESH)

    top, low = pl.ds(0, SHIFT), pl.ds(SHIFT, SHIFT)
    body, side, head = pl.ds(0, tile_cols), pl.ds(tile_cols, PAD), pl.ds(0, PAD)
    local = [
        pltpu.make_async_copy(s, d, local_sem.at[i])
        for i, (s, d) in enumerate(
            (
                (dom_hbm, dom_ref),
                (feat_hbm.at[low], ext_f.at[top, body]),
                (cot_hbm.at[low], ext_c.at[top, body]),
                (gain_hbm, gain_ref),
                (wqkv_hbm, wqkv_ref),
                (wproj_hbm, wproj_ref),
            )
        )
    ]
    for copy in local:
        copy.start()
    out32[:, :, 0:8, :] = jnp.zeros((2, tile_rows, 8, channels), F32)
    out32[:, :, tile_cols : tile_cols + PAD, :] = jnp.zeros((2, tile_rows, PAD, channels), F32)
    local[0].wait()
    dom = dom_ref[...].astype(F32)
    dom_out[...] = jnp.concatenate([dom, dom], 1)
    pl.semaphore_wait(barrier, len(greeted))

    def remote(src, dst, send, recv, target):
        return pltpu.make_async_remote_copy(
            src_ref=src,
            dst_ref=dst,
            send_sem=send,
            recv_sem=recv,
            device_id=target,
            device_id_type=pl.DeviceIdType.MESH,
        )

    up, left, corner = dev(r_up, me_c), dev(me_r, c_left), dev(r_up, c_left)
    pairs = ((feat_hbm, ext_f), (cot_hbm, ext_c))
    jobs = [(dom_out, ext_d.at[i], t) for i, t in enumerate((up, left, corner))]
    for b in range(blocks):
        block = pl.ds(b * PAD, PAD)
        jobs += [(s.at[top, block], d.at[low, block], up) for s, d in pairs]
    jobs += [(s.at[low, head], d.at[top, side], left) for s, d in pairs]
    jobs += [(s.at[top, head], d.at[low, side], corner) for s, d in pairs]
    halos = [
        remote(s, d, in_send.at[i], in_recv.at[i], t) for i, (s, d, t) in enumerate(jobs)
    ]
    for copy in halos:
        copy.start()
    for copy in local[1:]:
        copy.wait()
    gain = gain_ref[...]

    scale = head_dim ** (-0.5)
    half = 128
    per = half // head_dim
    hid = lax.broadcasted_iota(jnp.int32, (per, 1, half), 0)
    lid = lax.broadcasted_iota(jnp.int32, (per, 1, half), 2) // head_dim
    hm32 = jnp.where(hid == lid, 1.0, 0.0).astype(F32)
    hm = hm32.astype(BF16)
    kid = lax.broadcasted_iota(jnp.int32, (cells, cells), 0)
    qid = lax.broadcasted_iota(jnp.int32, (cells, cells), 1)
    mid = WIN * SHIFT
    row_diff = jnp.where((kid >= mid) != (qid >= mid), MASKED_SCORE, 0.0)
    kcol, qcol = lax.rem(kid, WIN) >= SHIFT, lax.rem(qid, WIN) >= SHIFT
    col_diff = jnp.where(kcol != qcol, MASKED_SCORE, 0.0)
    row_bias = row_diff * jnp.where(me_r == rows - 1, 1.0, 0.0)
    last_bias = row_bias + col_diff * jnp.where(me_c == cols - 1, 1.0, 0.0)

    for copy in halos[0:3]:
        copy.wait()
    lane = lax.broadcasted_iota(jnp.int32, (SHIFT, 2 * tile_cols), 1)
    dx[0:SHIFT, :] = jnp.where(lane < tile_cols, dom_out[SHIFT:, :], ext_d[1, SHIFT:, :])
    dx[SHIFT:, :] = jnp.where(lane < tile_cols, ext_d[0, 0:SHIFT, :], ext_d[2, 0:SHIFT, :])
    pick = lax.broadcasted_iota(jnp.int32, (WIN, 2 * tile_cols), 1) - lax.broadcasted_iota(
        jnp.int32, (WIN, 2 * tile_cols), 0
    )

    def attend(w, t):
        bias = (last_bias if w == windows - 1 else row_bias)[None]
        at = slice(t * half, (t + 1) * half)
        k_at = slice(channels + t * half, channels + (t + 1) * half)
        v_at = slice(2 * channels + t * half, 2 * channels + (t + 1) * half)
        q = proj[w, :, at]
        k = proj[w, :, k_at]
        v = proj[w, :, v_at]
        dc = dctx[w, :, at]
        kx = (k[None] * hm).reshape(per * cells, half)
        vx = (v[None] * hm).reshape(per * cells, half)
        s = nt(kx, q).reshape(per, cells, cells) + bias
        peak = jnp.max(s, 1, keepdims=True)
        e = jnp.exp2((s - peak) * (scale * LOG2E))
        p = e * (1.0 / jnp.sum(e, 1, keepdims=True))
        pb = p.astype(BF16).reshape(per * cells, cells)
        ctx[w, :, at] = tn(pb, vx).astype(BF16)
        dp = nt(vx, dc).astype(BF16).astype(F32).reshape(per, cells, cells)
        ds = p * (dp - jnp.sum(p * dp, 1, keepdims=True))
        dsb = ds.astype(BF16).reshape(per * cells, cells)
        dproj[w, :, at] = (tn(dsb, kx) * scale).astype(BF16)
        dk = nn(dsb, q).reshape(per, cells, half) * hm32
        dproj[w, :, k_at] = (jnp.sum(dk, 0) * scale).astype(BF16)
        dv = nn(pb, dc).reshape(per, cells, half) * hm32
        dproj[w, :, v_at] = jnp.sum(dv, 0).astype(BF16)

    gsum = jnp.zeros((WIN, channels), F32)
    both = pl.ds(0, 2)
    outs = []
    for b in range(blocks):
        for n in (0, 1) if b == 0 else (b + 1,):
            first = 3 + 2 * n
            for copy in halos[first : first + (2 if n < blocks else 4)]:
                copy.wait()
            block = slice(n * PAD, (n + 1) * PAD)
            xf[:, block, :] = ext_f[:, block, :].astype(F32)
            cf[:, block, :] = ext_c[:, block, :].astype(F32)
        mine_w = range(b * each, (b + 1) * each)
        for w in mine_w:
            for i in range(tile_rows):
                line = jnp.broadcast_to(dx[i : i + 1, :], (WIN, 2 * tile_cols))
                mask[w, i * WIN : (i + 1) * WIN, :] = jnp.sum(
                    jnp.where(pick == w * WIN + SHIFT, line, 0.0), -1, keepdims=True
                )
            at = slice(w * WIN + SHIFT, (w + 1) * WIN + SHIFT)
            x = xf[:, at, :].reshape(cells, channels)
            average = jnp.mean(x, -1, keepdims=True)
            centred = x - average
            variance = jnp.mean(centred * centred, -1, keepdims=True)
            inv = lax.rsqrt(variance + NORM_EPSILON)
            standard = centred * inv
            rstd[w] = inv
            xhat[w] = standard
            shifted[w] = (standard * gain).astype(BF16)
            c = cf[:, at, :].reshape(cells, channels)
            datt[w] = (c * mask[w]).astype(BF16)
        ws = slice(b * each, (b + 1) * each)
        count = each * cells
        s_chunk = shifted[ws].reshape(count, channels)
        d_chunk = datt[ws].reshape(count, channels)
        proj[ws] = nn(s_chunk, wqkv_ref[...]).astype(BF16).reshape(each, cells, 3 * channels)
        dctx[ws] = nt(d_chunk, wproj_ref[...]).astype(BF16).reshape(each, cells, channels)
        for w in mine_w:
            attend(w, 0)

    total = windows * cells
    hrows = channels // 2
    share = hrows // INNER
    wide = 4 * half
    other = dev(me_r, c_right)

    def half_sum(core, t):
        at = pl.ds(pl.multiple_of(core * hrows, hrows), hrows)
        left_s = shifted[:, :, at].reshape(total, hrows)
        right_d = datt[:, :, at].reshape(total, hrows)
        heads = [
            dproj[:, :, n * channels + t * half : n * channels + (t + 1) * half].reshape(total, half)
            for n in range(3)
        ]
        left_c = ctx[:, :, t * half : (t + 1) * half].reshape(total, half)
        return tn(left_s, jnp.concatenate(heads, 1)), tn(left_c, right_d)

    def core_start(t):
        sum_q, sum_p = half_sum(c_right, t)
        core_out[t, :, 0 : 3 * half] = sum_q.astype(BF16)
        core_out[t, :, 3 * half :] = sum_p.astype(BF16)
        copy = remote(core_out.at[t], core_in.at[t], core_send.at[t], core_recv.at[t], other)
        copy.start()
        sum_q, sum_p = half_sum(me_c, t)
        own_part[t, :, 0 : 3 * half] = sum_q
        own_part[t, :, 3 * half :] = sum_p
        return copy

    def chip_sum(j, t, extra):
        at = pl.ds(pl.multiple_of(j * share, share), share)
        sbuf[t, j, :, 0:wide] = (own_part[t, at, :] + core_in[t, at, :].astype(F32)).astype(BF16)
        if extra is not None:
            sbuf[t, j, :, wide:] = extra

    def span(extra):
        return pl.ds(0, wide if extra is None else wide + 128)

    def scatter_start(t, extra):
        copies = [None]
        for o in range(1, INNER):
            j = lax.rem(member + o, INNER)
            chip_sum(j, t, extra)
            copy = remote(
                sbuf.at[t, j, :, span(extra)],
                rbuf.at[t, o, :, span(extra)],
                rs_send.at[t, o],
                rs_recv.at[t, o],
                dev(peer(o), me_c),
            )
            copy.start()
            copies.append(copy)
        chip_sum(member, t, extra)
        return copies

    def scatter_end(t, extra, copies):
        width = wide if extra is None else wide + 128
        acc = sbuf[t, member, :, 0:width].astype(F32)
        for o in range(1, INNER):
            copies[o].wait()
            acc = acc + rbuf[t, o, :, 0:width].astype(F32)
        if outer > 1:
            obuf[t, :, 0:width] = acc.astype(BF16)
            spread = [
                remote(
                    obuf.at[t, :, span(extra)],
                    oin.at[t, o, :, span(extra)],
                    o_send.at[t, o],
                    o_recv.at[t, o],
                    dev(counterpart(o), me_c),
                )
                for o in range(1, outer)
            ]
            for copy in spread:
                copy.start()
            for o in range(1, outer):
                spread[o - 1].wait()
                acc = acc + oin[t, o, :, 0:width].astype(F32)
        return acc

    def gather_start(t, acc):
        mine = gsum_ref.at[t, me_c, member]
        mine[...] = acc[:, 0:wide].astype(BF16)
        copies = [
            remote(mine, mine, ag_send.at[t, o], ag_recv.at[t, o], dev(peer(o), me_c))
            for o in range(1, INNER)
        ]
        for copy in copies:
            copy.start()
        hand = remote(mine, mine, fw_send.at[t, 0], fw_recv.at[t, 0], other)
        hand.start()
        return copies, [hand]

    def gather_end(t, copies, handed):
        for o in range(1, INNER):
            copies[o - 1].wait()
            piece = gsum_ref.at[t, me_c, lax.rem(member + INNER - o, INNER)]
            copy = remote(piece, piece, fw_send.at[t, o], fw_recv.at[t, o], other)
            copy.start()
            handed.append(copy)

    early = core_start(0)
    for b in range(blocks):
        ws = slice(b * each, (b + 1) * each)
        mine_w = range(b * each, (b + 1) * each)
        for w in mine_w:
            attend(w, 1)
        p_chunk = dproj[ws].reshape(count, 3 * channels)
        dnormed = nt(p_chunk, wqkv_ref[...]).astype(BF16).astype(F32)
        c_chunk = ctx[ws].reshape(count, channels)
        attended = nn(c_chunk, wproj_ref[...]).astype(BF16).astype(F32)
        for u, w in enumerate(mine_w):
            at = slice(w * WIN + SHIFT, (w + 1) * WIN + SHIFT)
            dn = dnormed[u * cells : (u + 1) * cells]
            standard = xhat[w]
            gsum = gsum + jnp.sum((dn * standard).reshape(WIN, WIN, channels), 0)
            up_grad = dn * gain
            mean_g = jnp.mean(up_grad, -1, keepdims=True)
            mean_gx = jnp.mean(up_grad * standard, -1, keepdims=True)
            grad = rstd[w] * (up_grad - mean_g - standard * mean_gx)
            out32[1, :, at, :] = cf[:, at, :] + grad.reshape(WIN, WIN, channels)
            inside = mask[w] * attended[u * cells : (u + 1) * cells]
            out32[0, :, at, :] = xf[:, at, :] + inside.reshape(WIN, WIN, channels)
        block = slice(b * PAD, (b + 1) * PAD)
        outx[:, :, block, :] = out32[:, :, block, :].astype(BF16)
        area = pl.ds(b * PAD, PAD)
        copy = remote(
            outx.at[both, low, area],
            row_in.at[both, top, area],
            out_send.at[b],
            out_recv.at[b],
            dev(r_dn, me_c),
        )
        copy.start()
        outs.append(copy)
        if b == 0:
            early.wait()
            early_scatter = scatter_start(0, None)
        if b == blocks - 2:
            early_gather, early_hand = gather_start(0, scatter_end(0, None, early_scatter))

    late = core_start(1)
    gtile = jnp.concatenate([gsum[:, :half], gsum[:, half:]], 0)
    gcore_out[...] = gtile.astype(BF16)
    gain_copy = remote(gcore_out, gcore_in, core_send.at[2], core_recv.at[2], other)
    gain_copy.start()
    edge = slice(tile_cols, tile_cols + PAD)
    outx[:, :, edge, :] = out32[:, :, edge, :].astype(BF16)
    late.wait()
    gain_copy.wait()
    gchip = (gtile + gcore_in[...].astype(F32)).astype(BF16)
    late_scatter = scatter_start(1, gchip)
    last = [
        remote(
            outx.at[both, top, side],
            col_in,
            out_send.at[blocks],
            out_recv.at[blocks],
            dev(me_r, c_right),
        ),
        remote(
            outx.at[both, low, side],
            diag_in,
            out_send.at[blocks + 1],
            out_recv.at[blocks + 1],
            dev(r_dn, c_right),
        ),
    ]
    for copy in last:
        copy.start()
    outs += last
    gather_end(0, early_gather, early_hand)
    acc = scatter_end(1, gchip, late_scatter)
    late_gather, late_hand = gather_start(1, acc)
    gfold = jnp.concatenate([acc[0:WIN, wide:], acc[WIN:, wide:]], 1)
    ggain_ref[...] = jnp.sum(gfold, 0, keepdims=True)

    def give(i, src, dst):
        copy = pltpu.make_async_copy(src, dst, done_sem.at[i])
        copy.start()
        return copy

    results = [give(0, ggain_ref, ggain_hbm)]
    for copy in outs:
        copy.wait()
    col_id = lax.broadcasted_iota(jnp.int32, (SHIFT, PAD, channels), 1)
    for n, ref in enumerate((upd_ref, gfeat_ref)):
        ref[0:SHIFT, PAD:, :] = row_in[n, :, PAD:, :]
        ref[SHIFT:, PAD:, :] = outx[n, 0:SHIFT, PAD:tile_cols, :]
        ref[0:SHIFT, 0:PAD, :] = jnp.where(
            col_id < SHIFT, diag_in[n].astype(F32), row_in[n, :, 0:PAD, :].astype(F32)
        ).astype(BF16)
        ref[SHIFT:, 0:PAD, :] = jnp.where(
            col_id < SHIFT, col_in[n].astype(F32), outx[n, 0:SHIFT, 0:PAD, :].astype(F32)
        ).astype(BF16)
    results += [give(1, upd_ref, upd_hbm), give(2, gfeat_ref, gfeat_hbm)]

    gather_end(1, late_gather, late_hand)
    results.append(give(3, gsum_ref.at[both, me_c], gsum_hbm.at[both, me_c]))
    for copy in early_hand + late_hand:
        copy.wait()
    results.append(give(4, gsum_ref.at[both, c_right], gsum_hbm.at[both, c_right]))
    for copy in results:
        copy.wait()


def finish(
    upd_in,
    gfeat_in,
    gsum_in,
    ggain_in,
    upd,
    gfeat,
    gqkv,
    gproj,
    ggain,
    upd_mid,
    gfeat_mid,
    ggain_mid,
    sums,
    qkv32,
    proj32,
    in_sems,
    out_sems,
):
    channels = gqkv.shape[0]
    parts, halves, _, _, wide = sums.shape
    hrows = channels // halves
    half = wide // 4
    pairs = [(t, c) for t in range(parts) for c in range(halves)]

    def copies(jobs, sems):
        return [pltpu.make_async_copy(s, d, sems.at[i]) for i, (s, d) in enumerate(jobs)]

    reads = [(gsum_in.at[t, c], sums.at[t, c]) for t, c in pairs]
    reads += [(upd_in, upd_mid), (gfeat_in, gfeat_mid), (ggain_in, ggain_mid)]
    writes = [(qkv32, gqkv), (proj32, gproj)]
    writes += [(upd_mid, upd), (gfeat_mid, gfeat), (ggain_mid, ggain)]
    reads, writes = copies(reads, in_sems), copies(writes, out_sems)
    for copy in reads:
        copy.start()
    for n, (t, c) in enumerate(pairs):
        reads[n].wait()
        some = sums[t, c].reshape(hrows, wide).astype(F32)
        rows = slice(c * hrows, (c + 1) * hrows)
        for n in range(3):
            at = slice(n * channels + t * half, n * channels + (t + 1) * half)
            qkv32[rows, at] = some[:, n * half : (n + 1) * half]
        proj32[t * half : (t + 1) * half, rows] = some[:, 3 * half :]
    for n in range(2):
        writes[n].start()
    for n in range(3):
        reads[len(pairs) + n].wait()
        writes[2 + n].start()
    for copy in writes:
        copy.wait()


def on_device(features, cotangent, domain, qkv_weight, proj_weight, norm_gain):
    tile_rows, tile_cols, channels = features.shape
    rows, cols = lax.axis_size("row"), lax.axis_size("col")
    outer = rows // INNER
    windows, cells = tile_cols // WIN, WIN * WIN
    blocks = tile_cols // PAD
    piece = channels // 2 // INNER
    wide = 4 * 128
    ext = tile_cols + PAD
    vm = pltpu.VMEM
    dma = pltpu.SemaphoreType.DMA
    halos = 3 + 2 * blocks + 4
    aspec = pl.BlockSpec(memory_space=pltpu.HBM)
    results = pl.pallas_call(
        functools.partial(kernel, rows, cols),
        out_shape=(
            jax.ShapeDtypeStruct(features.shape, BF16),
            jax.ShapeDtypeStruct(features.shape, BF16),
            jax.ShapeDtypeStruct((2, 2, INNER, piece, wide), BF16),
            jax.ShapeDtypeStruct((1, channels), F32),
        ),
        in_specs=[aspec] * 6,
        out_specs=(aspec,) * 4,
        scratch_shapes=[
            vm(features.shape, BF16),
            vm(features.shape, BF16),
            vm((2, 2, INNER, piece, wide), BF16),
            vm((1, channels), F32),
            vm(qkv_weight.shape, BF16),
            vm(proj_weight.shape, BF16),
            vm((1, channels), F32),
            vm((tile_rows, tile_cols), jnp.int32),
            vm((tile_rows, 2 * tile_cols), F32),
            vm((tile_rows, ext, channels), BF16),
            vm((tile_rows, ext, channels), BF16),
            vm((3, tile_rows, 2 * tile_cols), F32),
            vm((tile_rows, ext, channels), F32),
            vm((tile_rows, ext, channels), F32),
            vm((tile_rows, 2 * tile_cols), F32),
            vm((windows, cells, 1), F32),
            vm((windows, cells, channels), F32),
            vm((windows, cells, 1), F32),
            vm((windows, cells, channels), BF16),
            vm((windows, cells, channels), BF16),
            vm((windows, cells, 3 * channels), BF16),
            vm((windows, cells, 3 * channels), BF16),
            vm((windows, cells, channels), BF16),
            vm((windows, cells, channels), BF16),
            vm((2, tile_rows, ext, channels), F32),
            vm((2, tile_rows, ext, channels), BF16),
            vm((2, SHIFT, tile_cols, channels), BF16),
            vm((2, SHIFT, PAD, channels), BF16),
            vm((2, SHIFT, PAD, channels), BF16),
            vm((2, channels // 2, wide), F32),
            vm((2, channels // 2, wide), BF16),
            vm((2, channels // 2, wide), BF16),
            vm((16, 128), BF16),
            vm((16, 128), BF16),
            vm((2, INNER, piece, wide + 128), BF16),
            vm((2, INNER, piece, wide + 128), BF16),
            vm((2, piece, wide + 128), BF16),
            vm((2, outer, piece, wide + 128), BF16),
            dma((6,)),
            dma((5,)),
            dma((halos,)),
            dma((halos,)),
            dma((blocks + 2,)),
            dma((blocks + 2,)),
            dma((3,)),
            dma((3,)),
            dma((2, INNER)),
            dma((2, INNER)),
            dma((2, outer)),
            dma((2, outer)),
            dma((2, INNER)),
            dma((2, INNER)),
            dma((2, INNER)),
            dma((2, INNER)),
        ],
        compiler_params=pltpu.CompilerParams(
            collective_id=0, has_side_effects=True, vmem_limit_bytes=60 * 1024 * 1024
        ),
    )(features, cotangent, domain, qkv_weight, proj_weight, norm_gain[None, :])
    outs = pl.pallas_call(
        finish,
        out_shape=(
            jax.ShapeDtypeStruct(features.shape, BF16),
            jax.ShapeDtypeStruct(features.shape, BF16),
            jax.ShapeDtypeStruct((channels, 3 * channels), F32),
            jax.ShapeDtypeStruct((channels, channels), F32),
            jax.ShapeDtypeStruct((1, channels), F32),
        ),
        in_specs=[aspec] * 4,
        out_specs=(aspec,) * 5,
        scratch_shapes=[
            vm(features.shape, BF16),
            vm(features.shape, BF16),
            vm((1, channels), F32),
            vm((2, 2, INNER, piece, wide), BF16),
            vm((channels, 3 * channels), F32),
            vm((channels, channels), F32),
            dma((7,)),
            dma((5,)),
        ],
        compiler_params=pltpu.CompilerParams(vmem_limit_bytes=60 * 1024 * 1024),
    )(*results)
    return (outs[0], outs[1], outs[2], outs[3], outs[4].reshape(channels))


def solution(mesh):
    return jax.shard_map(
        on_device,
        mesh=mesh,
        in_specs=(
            P(("grp", "row"), "col", None),
            P(("grp", "row"), "col", None),
            P(("grp", "row"), "col"),
            P(),
            P(),
            P(),
        ),
        out_specs=(
            P(("grp", "row"), "col", None),
            P(("grp", "row"), "col", None),
            P("grp", None),
            P("grp", None),
            P("grp"),
        ),
        check_vma=False,
    )
```

```python
import functools

import jax
import jax.numpy as jnp
from jax import lax
from jax.experimental import pallas as pl
from jax.experimental.pallas import tpu as pltpu
from jax.sharding import PartitionSpec as P

HEADS = 8
WIN = 8
SHIFT = 4
NORM_EPSILON = 1e-05
MASKED_SCORE = -1e30
LOG2E = 1.4426950408889634
INNER = 8
PAD = 16

F32 = jnp.float32
BF16 = jnp.bfloat16


def nn(a, b):
    return lax.dot_general(a, b, (((1,), (0,)), ((), ())), preferred_element_type=F32)


def nt(a, b):
    return lax.dot_general(a, b, (((1,), (1,)), ((), ())), preferred_element_type=F32)


def tn(a, b):
    return lax.dot_general(a, b, (((0,), (0,)), ((), ())), preferred_element_type=F32)


def kernel(
    rows,
    cols,
    feat_hbm,
    cot_hbm,
    dom_hbm,
    wqkv_hbm,
    wproj_hbm,
    gain_hbm,
    upd_hbm,
    gfeat_hbm,
    gsum_hbm,
    ggain_hbm,
    upd_ref,
    gfeat_ref,
    gsum_ref,
    ggain_ref,
    wqkv_ref,
    wproj_ref,
    gain_ref,
    dom_ref,
    dom_out,
    ext_f,
    ext_c,
    ext_d,
    xf,
    cf,
    dx,
    mask,
    xhat,
    rstd,
    shifted,
    datt,
    proj,
    dproj,
    ctx,
    dctx,
    out32,
    outx,
    row_in,
    col_in,
    diag_in,
    own_part,
    core_out,
    core_in,
    gcore_out,
    gcore_in,
    sbuf,
    rbuf,
    obuf,
    oin,
    local_sem,
    done_sem,
    in_send,
    in_recv,
    out_send,
    out_recv,
    core_send,
    core_recv,
    rs_send,
    rs_recv,
    o_send,
    o_recv,
    ag_send,
    ag_recv,
    fw_send,
    fw_recv,
):
    tile_rows, tile_cols, channels = feat_hbm.shape
    windows = tile_cols // WIN
    cells = WIN * WIN
    head_dim = channels // HEADS
    blocks = tile_cols // PAD
    chunks = 2
    each = windows // chunks
    reach = blocks // chunks
    outer = rows // INNER
    me_r = lax.axis_index("row")
    me_c = lax.axis_index("col")
    r_up = lax.rem(me_r + rows - 1, rows)
    r_dn = lax.rem(me_r + 1, rows)
    c_left = lax.rem(me_c + cols - 1, cols)
    c_right = lax.rem(me_c + 1, cols)
    group = me_r // INNER
    member = lax.rem(me_r, INNER)

    def dev(r, c):
        return {"row": r, "col": c}

    def peer(o):
        return group * INNER + lax.rem(member + o, INNER)

    def counterpart(o):
        return lax.rem(group + o, outer) * INNER + member

    barrier = pltpu.get_barrier_semaphore()
    greeted = [
        dev(r_up, me_c),
        dev(r_dn, me_c),
        dev(me_r, c_left),
        dev(r_up, c_left),
        dev(r_dn, c_right),
    ]
    greeted += [dev(peer(o), me_c) for o in range(1, INNER)]
    greeted += [dev(counterpart(o), me_c) for o in range(1, outer)]
    for target in greeted:
        pl.semaphore_signal(barrier, inc=1, device_id=target, device_id_type=pl.DeviceIdType.MESH)

    top, low = pl.ds(0, SHIFT), pl.ds(SHIFT, SHIFT)
    body, side, head = pl.ds(0, tile_cols), pl.ds(tile_cols, PAD), pl.ds(0, PAD)
    local = [
        pltpu.make_async_copy(s, d, local_sem.at[i])
        for i, (s, d) in enumerate(
            (
                (dom_hbm, dom_ref),
                (feat_hbm.at[low], ext_f.at[top, body]),
                (cot_hbm.at[low], ext_c.at[top, body]),
                (gain_hbm, gain_ref),
                (wqkv_hbm, wqkv_ref),
                (wproj_hbm, wproj_ref),
            )
        )
    ]
    for copy in local:
        copy.start()
    out32[:, :, 0:8, :] = jnp.zeros((2, tile_rows, 8, channels), F32)
    out32[:, :, tile_cols : tile_cols + PAD, :] = jnp.zeros((2, tile_rows, PAD, channels), F32)
    local[0].wait()
    dom = dom_ref[...].astype(F32)
    dom_out[...] = jnp.concatenate([dom, dom], 1)
    pl.semaphore_wait(barrier, len(greeted))

    def remote(src, dst, send, recv, target):
        return pltpu.make_async_remote_copy(
            src_ref=src,
            dst_ref=dst,
            send_sem=send,
            recv_sem=recv,
            device_id=target,
            device_id_type=pl.DeviceIdType.MESH,
        )

    up, left, corner = dev(r_up, me_c), dev(me_r, c_left), dev(r_up, c_left)
    pairs = ((feat_hbm, ext_f), (cot_hbm, ext_c))
    jobs = [(dom_out, ext_d.at[i], t) for i, t in enumerate((up, left, corner))]
    for b in range(blocks):
        block = pl.ds(b * PAD, PAD)
        jobs += [(s.at[top, block], d.at[low, block], up) for s, d in pairs]
    jobs += [(s.at[low, head], d.at[top, side], left) for s, d in pairs]
    jobs += [(s.at[top, head], d.at[low, side], corner) for s, d in pairs]
    halos = [
        remote(s, d, in_send.at[i], in_recv.at[i], t) for i, (s, d, t) in enumerate(jobs)
    ]
    for copy in halos:
        copy.start()
    for copy in local[1:]:
        copy.wait()
    gain = gain_ref[...]

    scale = head_dim ** (-0.5)
    half = 128
    per = half // head_dim
    hid = lax.broadcasted_iota(jnp.int32, (per, 1, half), 0)
    lid = lax.broadcasted_iota(jnp.int32, (per, 1, half), 2) // head_dim
    hm32 = jnp.where(hid == lid, 1.0, 0.0).astype(F32)
    hm = hm32.astype(BF16)
    kid = lax.broadcasted_iota(jnp.int32, (cells, cells), 0)
    qid = lax.broadcasted_iota(jnp.int32, (cells, cells), 1)
    mid = WIN * SHIFT
    row_diff = jnp.where((kid >= mid) != (qid >= mid), MASKED_SCORE, 0.0)
    kcol, qcol = lax.rem(kid, WIN) >= SHIFT, lax.rem(qid, WIN) >= SHIFT
    col_diff = jnp.where(kcol != qcol, MASKED_SCORE, 0.0)
    row_bias = row_diff * jnp.where(me_r == rows - 1, 1.0, 0.0)
    last_bias = row_bias + col_diff * jnp.where(me_c == cols - 1, 1.0, 0.0)

    for copy in halos[0:3]:
        copy.wait()
    lane = lax.broadcasted_iota(jnp.int32, (SHIFT, 2 * tile_cols), 1)
    dx[0:SHIFT, :] = jnp.where(lane < tile_cols, dom_out[SHIFT:, :], ext_d[1, SHIFT:, :])
    dx[SHIFT:, :] = jnp.where(lane < tile_cols, ext_d[0, 0:SHIFT, :], ext_d[2, 0:SHIFT, :])
    pick = lax.broadcasted_iota(jnp.int32, (WIN, 2 * tile_cols), 1) - lax.broadcasted_iota(
        jnp.int32, (WIN, 2 * tile_cols), 0
    )

    def attend(ws, t):
        at = slice(t * half, (t + 1) * half)
        k_at = slice(channels + t * half, channels + (t + 1) * half)
        v_at = slice(2 * channels + t * half, 2 * channels + (t + 1) * half)
        heads = (per, cells, cells)
        flat = (per * cells, cells)
        kx = [(proj[w, :, k_at][None] * hm).reshape(per * cells, half) for w in ws]
        vx = [(proj[w, :, v_at][None] * hm).reshape(per * cells, half) for w in ws]
        s = [nt(k, proj[w, :, at]).reshape(heads) for k, w in zip(kx, ws)]
        dp = [nt(v, dctx[w, :, at]).astype(BF16).astype(F32).reshape(heads) for v, w in zip(vx, ws)]
        s = [x + (last_bias if w == windows - 1 else row_bias)[None] for x, w in zip(s, ws)]
        e = [jnp.exp2((x - jnp.max(x, 1, keepdims=True)) * (scale * LOG2E)) for x in s]
        p = [x * (1.0 / jnp.sum(x, 1, keepdims=True)) for x in e]
        pb = [x.astype(BF16).reshape(flat) for x in p]
        ds = [x * (y - jnp.sum(x * y, 1, keepdims=True)) for x, y in zip(p, dp)]
        dsb = [x.astype(BF16).reshape(flat) for x in ds]
        for n, w in enumerate(ws):
            ctx[w, :, at] = tn(pb[n], vx[n]).astype(BF16)
        for n, w in enumerate(ws):
            dv = nn(pb[n], dctx[w, :, at]).reshape(per, cells, half) * hm32
            dproj[w, :, v_at] = jnp.sum(dv, 0).astype(BF16)
        for n, w in enumerate(ws):
            dproj[w, :, at] = (tn(dsb[n], kx[n]) * scale).astype(BF16)
        for n, w in enumerate(ws):
            dk = nn(dsb[n], proj[w, :, at]).reshape(per, cells, half) * hm32
            dproj[w, :, k_at] = (jnp.sum(dk, 0) * scale).astype(BF16)

    gsum = jnp.zeros((WIN, channels), F32)
    both = pl.ds(0, 2)
    outs = []
    for b in range(chunks):
        for n in range(b * reach + (b > 0), (b + 1) * reach + 1):
            first = 3 + 2 * n
            for copy in halos[first : first + (2 if n < blocks else 4)]:
                copy.wait()
            block = slice(n * PAD, (n + 1) * PAD)
            xf[:, block, :] = ext_f[:, block, :].astype(F32)
            cf[:, block, :] = ext_c[:, block, :].astype(F32)
        mine_w = range(b * each, (b + 1) * each)
        for w in mine_w:
            for i in range(tile_rows):
                line = jnp.broadcast_to(dx[i : i + 1, :], (WIN, 2 * tile_cols))
                mask[w, i * WIN : (i + 1) * WIN, :] = jnp.sum(
                    jnp.where(pick == w * WIN + SHIFT, line, 0.0), -1, keepdims=True
                )
            at = slice(w * WIN + SHIFT, (w + 1) * WIN + SHIFT)
            x = xf[:, at, :].reshape(cells, channels)
            average = jnp.mean(x, -1, keepdims=True)
            centred = x - average
            variance = jnp.mean(centred * centred, -1, keepdims=True)
            inv = lax.rsqrt(variance + NORM_EPSILON)
            standard = centred * inv
            rstd[w] = inv
            xhat[w] = standard
            shifted[w] = (standard * gain).astype(BF16)
            c = cf[:, at, :].reshape(cells, channels)
            datt[w] = (c * mask[w]).astype(BF16)
        ws = slice(b * each, (b + 1) * each)
        count = each * cells
        s_chunk = shifted[ws].reshape(count, channels)
        d_chunk = datt[ws].reshape(count, channels)
        proj[ws] = nn(s_chunk, wqkv_ref[...]).astype(BF16).reshape(each, cells, 3 * channels)
        dctx[ws] = nt(d_chunk, wproj_ref[...]).astype(BF16).reshape(each, cells, channels)
        attend(mine_w, 0)

    total = windows * cells
    hrows = channels // 2
    share = hrows // INNER
    wide = 4 * half
    other = dev(me_r, c_right)

    def half_sum(core, t):
        at = pl.ds(pl.multiple_of(core * hrows, hrows), hrows)
        left_s = shifted[:, :, at].reshape(total, hrows)
        right_d = datt[:, :, at].reshape(total, hrows)
        heads = [
            dproj[:, :, n * channels + t * half : n * channels + (t + 1) * half].reshape(total, half)
            for n in range(3)
        ]
        left_c = ctx[:, :, t * half : (t + 1) * half].reshape(total, half)
        return tn(left_s, jnp.concatenate(heads, 1)), tn(left_c, right_d)

    def core_start(t):
        sum_q, sum_p = half_sum(c_right, t)
        core_out[t, :, 0 : 3 * half] = sum_q.astype(BF16)
        core_out[t, :, 3 * half :] = sum_p.astype(BF16)
        copy = remote(core_out.at[t], core_in.at[t], core_send.at[t], core_recv.at[t], other)
        copy.start()
        sum_q, sum_p = half_sum(me_c, t)
        own_part[t, :, 0 : 3 * half] = sum_q
        own_part[t, :, 3 * half :] = sum_p
        return copy

    def chip_sum(j, t, extra):
        at = pl.ds(pl.multiple_of(j * share, share), share)
        sbuf[t, j, :, 0:wide] = (own_part[t, at, :] + core_in[t, at, :].astype(F32)).astype(BF16)
        if extra is not None:
            sbuf[t, j, :, wide:] = extra

    def span(extra):
        return pl.ds(0, wide if extra is None else wide + 128)

    def scatter_start(t, extra):
        copies = [None]
        for o in range(1, INNER):
            j = lax.rem(member + o, INNER)
            chip_sum(j, t, extra)
            copy = remote(
                sbuf.at[t, j, :, span(extra)],
                rbuf.at[t, o, :, span(extra)],
                rs_send.at[t, o],
                rs_recv.at[t, o],
                dev(peer(o), me_c),
            )
            copy.start()
            copies.append(copy)
        chip_sum(member, t, extra)
        return copies

    def scatter_end(t, extra, copies):
        width = wide if extra is None else wide + 128
        acc = sbuf[t, member, :, 0:width].astype(F32)
        for o in range(1, INNER):
            copies[o].wait()
            acc = acc + rbuf[t, o, :, 0:width].astype(F32)
        if outer > 1:
            obuf[t, :, 0:width] = acc.astype(BF16)
            spread = [
                remote(
                    obuf.at[t, :, span(extra)],
                    oin.at[t, o, :, span(extra)],
                    o_send.at[t, o],
                    o_recv.at[t, o],
                    dev(counterpart(o), me_c),
                )
                for o in range(1, outer)
            ]
            for copy in spread:
                copy.start()
            for o in range(1, outer):
                spread[o - 1].wait()
                acc = acc + oin[t, o, :, 0:width].astype(F32)
        return acc

    def gather_start(t, acc):
        mine = gsum_ref.at[t, me_c, member]
        mine[...] = acc[:, 0:wide].astype(BF16)
        copies = [
            remote(mine, mine, ag_send.at[t, o], ag_recv.at[t, o], dev(peer(o), me_c))
            for o in range(1, INNER)
        ]
        for copy in copies:
            copy.start()
        hand = remote(mine, mine, fw_send.at[t, 0], fw_recv.at[t, 0], other)
        hand.start()
        return copies, [hand]

    def gather_end(t, copies, handed):
        for o in range(1, INNER):
            copies[o - 1].wait()
            piece = gsum_ref.at[t, me_c, lax.rem(member + INNER - o, INNER)]
            copy = remote(piece, piece, fw_send.at[t, o], fw_recv.at[t, o], other)
            copy.start()
            handed.append(copy)

    early = core_start(0)
    for b in range(chunks):
        ws = slice(b * each, (b + 1) * each)
        mine_w = range(b * each, (b + 1) * each)
        attend(mine_w, 1)
        if b == 0:
            early.wait()
            early_scatter = scatter_start(0, None)
        if b == chunks - 1:
            early_gather, early_hand = gather_start(0, scatter_end(0, None, early_scatter))
        p_chunk = dproj[ws].reshape(count, 3 * channels)
        dnormed = nt(p_chunk, wqkv_ref[...]).astype(BF16).astype(F32)
        c_chunk = ctx[ws].reshape(count, channels)
        attended = nn(c_chunk, wproj_ref[...]).astype(BF16).astype(F32)
        for u, w in enumerate(mine_w):
            at = slice(w * WIN + SHIFT, (w + 1) * WIN + SHIFT)
            dn = dnormed[u * cells : (u + 1) * cells]
            standard = xhat[w]
            gsum = gsum + jnp.sum((dn * standard).reshape(WIN, WIN, channels), 0)
            up_grad = dn * gain
            mean_g = jnp.mean(up_grad, -1, keepdims=True)
            mean_gx = jnp.mean(up_grad * standard, -1, keepdims=True)
            grad = rstd[w] * (up_grad - mean_g - standard * mean_gx)
            out32[1, :, at, :] = cf[:, at, :] + grad.reshape(WIN, WIN, channels)
            inside = mask[w] * attended[u * cells : (u + 1) * cells]
            out32[0, :, at, :] = xf[:, at, :] + inside.reshape(WIN, WIN, channels)
        block = slice(b * reach * PAD, (b + 1) * reach * PAD)
        outx[:, :, block, :] = out32[:, :, block, :].astype(BF16)
        area = pl.ds(b * reach * PAD, reach * PAD)
        copy = remote(
            outx.at[both, low, area],
            row_in.at[both, top, area],
            out_send.at[b],
            out_recv.at[b],
            dev(r_dn, me_c),
        )
        copy.start()
        outs.append(copy)

    late = core_start(1)
    gtile = jnp.concatenate([gsum[:, :half], gsum[:, half:]], 0)
    gcore_out[...] = gtile.astype(BF16)
    gain_copy = remote(gcore_out, gcore_in, core_send.at[2], core_recv.at[2], other)
    gain_copy.start()
    edge = slice(tile_cols, tile_cols + PAD)
    outx[:, :, edge, :] = out32[:, :, edge, :].astype(BF16)
    late.wait()
    gain_copy.wait()
    gchip = (gtile + gcore_in[...].astype(F32)).astype(BF16)
    late_scatter = scatter_start(1, gchip)
    last = [
        remote(
            outx.at[both, top, side],
            col_in,
            out_send.at[blocks],
            out_recv.at[blocks],
            dev(me_r, c_right),
        ),
        remote(
            outx.at[both, low, side],
            diag_in,
            out_send.at[blocks + 1],
            out_recv.at[blocks + 1],
            dev(r_dn, c_right),
        ),
    ]
    for copy in last:
        copy.start()
    outs += last
    gather_end(0, early_gather, early_hand)
    acc = scatter_end(1, gchip, late_scatter)
    late_gather, late_hand = gather_start(1, acc)
    gfold = jnp.concatenate([acc[0:WIN, wide:], acc[WIN:, wide:]], 1)
    ggain_ref[...] = jnp.sum(gfold, 0, keepdims=True)

    def give(i, src, dst):
        copy = pltpu.make_async_copy(src, dst, done_sem.at[i])
        copy.start()
        return copy

    results = [give(0, ggain_ref, ggain_hbm)]
    for copy in outs:
        copy.wait()
    col_id = lax.broadcasted_iota(jnp.int32, (SHIFT, PAD, channels), 1)
    for n, ref in enumerate((upd_ref, gfeat_ref)):
        ref[0:SHIFT, PAD:, :] = row_in[n, :, PAD:, :]
        ref[SHIFT:, PAD:, :] = outx[n, 0:SHIFT, PAD:tile_cols, :]
        ref[0:SHIFT, 0:PAD, :] = jnp.where(
            col_id < SHIFT, diag_in[n].astype(F32), row_in[n, :, 0:PAD, :].astype(F32)
        ).astype(BF16)
        ref[SHIFT:, 0:PAD, :] = jnp.where(
            col_id < SHIFT, col_in[n].astype(F32), outx[n, 0:SHIFT, 0:PAD, :].astype(F32)
        ).astype(BF16)
    results += [give(1, upd_ref, upd_hbm), give(2, gfeat_ref, gfeat_hbm)]

    gather_end(1, late_gather, late_hand)
    results.append(give(3, gsum_ref.at[both, me_c], gsum_hbm.at[both, me_c]))
    for copy in early_hand + late_hand:
        copy.wait()
    results.append(give(4, gsum_ref.at[both, c_right], gsum_hbm.at[both, c_right]))
    for copy in results:
        copy.wait()


def finish(
    upd_in,
    gfeat_in,
    gsum_in,
    ggain_in,
    upd,
    gfeat,
    gqkv,
    gproj,
    ggain,
    upd_mid,
    gfeat_mid,
    ggain_mid,
    sums,
    qkv32,
    proj32,
    in_sems,
    out_sems,
):
    channels = gqkv.shape[0]
    parts, halves, _, _, wide = sums.shape
    hrows = channels // halves
    half = wide // 4
    pairs = [(t, c) for t in range(parts) for c in range(halves)]

    def copies(jobs, sems):
        return [pltpu.make_async_copy(s, d, sems.at[i]) for i, (s, d) in enumerate(jobs)]

    reads = [(gsum_in.at[t, c], sums.at[t, c]) for t, c in pairs]
    reads += [(upd_in, upd_mid), (gfeat_in, gfeat_mid), (ggain_in, ggain_mid)]
    writes = [(qkv32, gqkv), (proj32, gproj)]
    writes += [(upd_mid, upd), (gfeat_mid, gfeat), (ggain_mid, ggain)]
    reads, writes = copies(reads, in_sems), copies(writes, out_sems)
    for copy in reads:
        copy.start()
    for n, (t, c) in enumerate(pairs):
        reads[n].wait()
        some = sums[t, c].reshape(hrows, wide).astype(F32)
        rows = slice(c * hrows, (c + 1) * hrows)
        for n in range(3):
            at = slice(n * channels + t * half, n * channels + (t + 1) * half)
            qkv32[rows, at] = some[:, n * half : (n + 1) * half]
        proj32[t * half : (t + 1) * half, rows] = some[:, 3 * half :]
    for n in range(2):
        writes[n].start()
    for n in range(3):
        reads[len(pairs) + n].wait()
        writes[2 + n].start()
    for copy in writes:
        copy.wait()


def on_device(features, cotangent, domain, qkv_weight, proj_weight, norm_gain):
    tile_rows, tile_cols, channels = features.shape
    rows, cols = lax.axis_size("row"), lax.axis_size("col")
    outer = rows // INNER
    windows, cells = tile_cols // WIN, WIN * WIN
    blocks = tile_cols // PAD
    piece = channels // 2 // INNER
    wide = 4 * 128
    ext = tile_cols + PAD
    vm = pltpu.VMEM
    dma = pltpu.SemaphoreType.DMA
    halos = 3 + 2 * blocks + 4
    aspec = pl.BlockSpec(memory_space=pltpu.HBM)
    results = pl.pallas_call(
        functools.partial(kernel, rows, cols),
        out_shape=(
            jax.ShapeDtypeStruct(features.shape, BF16),
            jax.ShapeDtypeStruct(features.shape, BF16),
            jax.ShapeDtypeStruct((2, 2, INNER, piece, wide), BF16),
            jax.ShapeDtypeStruct((1, channels), F32),
        ),
        in_specs=[aspec] * 6,
        out_specs=(aspec,) * 4,
        scratch_shapes=[
            vm(features.shape, BF16),
            vm(features.shape, BF16),
            vm((2, 2, INNER, piece, wide), BF16),
            vm((1, channels), F32),
            vm(qkv_weight.shape, BF16),
            vm(proj_weight.shape, BF16),
            vm((1, channels), F32),
            vm((tile_rows, tile_cols), jnp.int32),
            vm((tile_rows, 2 * tile_cols), F32),
            vm((tile_rows, ext, channels), BF16),
            vm((tile_rows, ext, channels), BF16),
            vm((3, tile_rows, 2 * tile_cols), F32),
            vm((tile_rows, ext, channels), F32),
            vm((tile_rows, ext, channels), F32),
            vm((tile_rows, 2 * tile_cols), F32),
            vm((windows, cells, 1), F32),
            vm((windows, cells, channels), F32),
            vm((windows, cells, 1), F32),
            vm((windows, cells, channels), BF16),
            vm((windows, cells, channels), BF16),
            vm((windows, cells, 3 * channels), BF16),
            vm((windows, cells, 3 * channels), BF16),
            vm((windows, cells, channels), BF16),
            vm((windows, cells, channels), BF16),
            vm((2, tile_rows, ext, channels), F32),
            vm((2, tile_rows, ext, channels), BF16),
            vm((2, SHIFT, tile_cols, channels), BF16),
            vm((2, SHIFT, PAD, channels), BF16),
            vm((2, SHIFT, PAD, channels), BF16),
            vm((2, channels // 2, wide), F32),
            vm((2, channels // 2, wide), BF16),
            vm((2, channels // 2, wide), BF16),
            vm((16, 128), BF16),
            vm((16, 128), BF16),
            vm((2, INNER, piece, wide + 128), BF16),
            vm((2, INNER, piece, wide + 128), BF16),
            vm((2, piece, wide + 128), BF16),
            vm((2, outer, piece, wide + 128), BF16),
            dma((6,)),
            dma((5,)),
            dma((halos,)),
            dma((halos,)),
            dma((blocks + 2,)),
            dma((blocks + 2,)),
            dma((3,)),
            dma((3,)),
            dma((2, INNER)),
            dma((2, INNER)),
            dma((2, outer)),
            dma((2, outer)),
            dma((2, INNER)),
            dma((2, INNER)),
            dma((2, INNER)),
            dma((2, INNER)),
        ],
        compiler_params=pltpu.CompilerParams(
            collective_id=0, has_side_effects=True, vmem_limit_bytes=60 * 1024 * 1024
        ),
    )(features, cotangent, domain, qkv_weight, proj_weight, norm_gain[None, :])
    outs = pl.pallas_call(
        finish,
        out_shape=(
            jax.ShapeDtypeStruct(features.shape, BF16),
            jax.ShapeDtypeStruct(features.shape, BF16),
            jax.ShapeDtypeStruct((channels, 3 * channels), F32),
            jax.ShapeDtypeStruct((channels, channels), F32),
            jax.ShapeDtypeStruct((1, channels), F32),
        ),
        in_specs=[aspec] * 4,
        out_specs=(aspec,) * 5,
        scratch_shapes=[
            vm(features.shape, BF16),
            vm(features.shape, BF16),
            vm((1, channels), F32),
            vm((2, 2, INNER, piece, wide), BF16),
            vm((channels, 3 * channels), F32),
            vm((channels, channels), F32),
            dma((7,)),
            dma((5,)),
        ],
        compiler_params=pltpu.CompilerParams(vmem_limit_bytes=60 * 1024 * 1024),
    )(*results)
    return (outs[0], outs[1], outs[2], outs[3], outs[4].reshape(channels))


def solution(mesh):
    return jax.shard_map(
        on_device,
        mesh=mesh,
        in_specs=(
            P(("grp", "row"), "col", None),
            P(("grp", "row"), "col", None),
            P(("grp", "row"), "col"),
            P(),
            P(),
            P(),
        ),
        out_specs=(
            P(("grp", "row"), "col", None),
            P(("grp", "row"), "col", None),
            P("grp", None),
            P("grp", None),
            P("grp"),
        ),
        check_vma=False,
    )
```

```python
import functools

import jax
import jax.numpy as jnp
from jax import lax
from jax.experimental import pallas as pl
from jax.experimental.pallas import tpu as pltpu
from jax.sharding import PartitionSpec as P

HEADS = 8
WIN = 8
SHIFT = 4
NORM_EPSILON = 1e-05
MASKED_SCORE = -1e30
LOG2E = 1.4426950408889634
INNER = 8
PAD = 16

F32 = jnp.float32
BF16 = jnp.bfloat16


def nn(a, b):
    return lax.dot_general(a, b, (((1,), (0,)), ((), ())), preferred_element_type=F32)


def nt(a, b):
    return lax.dot_general(a, b, (((1,), (1,)), ((), ())), preferred_element_type=F32)


def tn(a, b):
    return lax.dot_general(a, b, (((0,), (0,)), ((), ())), preferred_element_type=F32)


def kernel(
    rows,
    cols,
    feat_hbm,
    cot_hbm,
    dom_hbm,
    wqkv_hbm,
    wproj_hbm,
    gain_hbm,
    upd_hbm,
    gfeat_hbm,
    gsum_hbm,
    ggain_hbm,
    upd_ref,
    gfeat_ref,
    gsum_ref,
    ggain_ref,
    wqkv_ref,
    wproj_ref,
    gain_ref,
    dom_ref,
    dom_out,
    own,
    ext,
    ext_d,
    xf,
    cf,
    dx,
    mask,
    xhat,
    rstd,
    shifted,
    datt,
    proj,
    dproj,
    ctx,
    dctx,
    out32,
    outx,
    row_in,
    col_in,
    diag_in,
    own_part,
    core_out,
    core_in,
    gcore_out,
    gcore_in,
    sbuf,
    rbuf,
    obuf,
    oin,
    local_sem,
    done_sem,
    in_send,
    in_recv,
    out_send,
    out_recv,
    core_send,
    core_recv,
    rs_send,
    rs_recv,
    o_send,
    o_recv,
    ag_send,
    ag_recv,
    fw_send,
    fw_recv,
):
    tile_rows, tile_cols, channels = feat_hbm.shape
    windows = tile_cols // WIN
    cells = WIN * WIN
    head_dim = channels // HEADS
    blocks = tile_cols // PAD
    chunks = 2
    each = windows // chunks
    reach = blocks // chunks
    outer = rows // INNER
    me_r = lax.axis_index("row")
    me_c = lax.axis_index("col")
    r_up = lax.rem(me_r + rows - 1, rows)
    r_dn = lax.rem(me_r + 1, rows)
    c_left = lax.rem(me_c + cols - 1, cols)
    c_right = lax.rem(me_c + 1, cols)
    group = me_r // INNER
    member = lax.rem(me_r, INNER)

    def dev(r, c):
        return {"row": r, "col": c}

    def peer(o):
        return group * INNER + lax.rem(member + o, INNER)

    def counterpart(o):
        return lax.rem(group + o, outer) * INNER + member

    barrier = pltpu.get_barrier_semaphore()
    greeted = [
        dev(r_up, me_c),
        dev(r_dn, me_c),
        dev(me_r, c_left),
        dev(r_up, c_left),
        dev(r_dn, c_right),
    ]
    greeted += [dev(peer(o), me_c) for o in range(1, INNER)]
    greeted += [dev(counterpart(o), me_c) for o in range(1, outer)]
    for target in greeted:
        pl.semaphore_signal(barrier, inc=1, device_id=target, device_id_type=pl.DeviceIdType.MESH)

    top, low = pl.ds(0, SHIFT), pl.ds(SHIFT, SHIFT)
    body, side, head = pl.ds(0, tile_cols), pl.ds(tile_cols, PAD), pl.ds(0, PAD)
    local = [
        pltpu.make_async_copy(s, d, local_sem.at[i])
        for i, (s, d) in enumerate(
            (
                (dom_hbm, dom_ref),
                (feat_hbm, own.at[0]),
                (cot_hbm, own.at[1]),
                (gain_hbm, gain_ref),
                (wqkv_hbm, wqkv_ref),
                (wproj_hbm, wproj_ref),
            )
        )
    ]
    for copy in local:
        copy.start()
    out32[:, :, 0:8, :] = jnp.zeros((2, tile_rows, 8, channels), F32)
    out32[:, :, tile_cols : tile_cols + PAD, :] = jnp.zeros((2, tile_rows, PAD, channels), F32)
    local[0].wait()
    dom = dom_ref[...].astype(F32)
    dom_out[...] = jnp.concatenate([dom, dom], 1)
    for copy in local[1:3]:
        copy.wait()
    pl.semaphore_wait(barrier, len(greeted))

    def remote(src, dst, send, recv, target):
        return pltpu.make_async_remote_copy(
            src_ref=src,
            dst_ref=dst,
            send_sem=send,
            recv_sem=recv,
            device_id=target,
            device_id_type=pl.DeviceIdType.MESH,
        )

    up, left, corner = dev(r_up, me_c), dev(me_r, c_left), dev(r_up, c_left)
    both = pl.ds(0, 2)
    jobs = [(dom_out, ext_d.at[i], t) for i, t in enumerate((up, left, corner))]
    cuts = [0] + [(b * reach + 1) * PAD for b in range(1, chunks)] + [tile_cols]
    for first, end in zip(cuts, cuts[1:]):
        area = pl.ds(first, end - first)
        jobs.append((own.at[both, top, area], ext.at[both, low, area], up))
    jobs.append((own.at[both, low, head], ext.at[both, top, side], left))
    jobs.append((own.at[both, top, head], ext.at[both, low, side], corner))
    halos = [
        remote(s, d, in_send.at[i], in_recv.at[i], t) for i, (s, d, t) in enumerate(jobs)
    ]
    for copy in halos:
        copy.start()
    xf[0:SHIFT, 0:tile_cols, :] = own[0, SHIFT:, :, :].astype(F32)
    cf[0:SHIFT, 0:tile_cols, :] = own[1, SHIFT:, :, :].astype(F32)
    for copy in local[3:]:
        copy.wait()
    gain = gain_ref[...]

    scale = head_dim ** (-0.5)
    half = 128
    per = half // head_dim
    hid = lax.broadcasted_iota(jnp.int32, (per, 1, half), 0)
    lid = lax.broadcasted_iota(jnp.int32, (per, 1, half), 2) // head_dim
    hm32 = jnp.where(hid == lid, 1.0, 0.0).astype(F32)
    hm = hm32.astype(BF16)
    kid = lax.broadcasted_iota(jnp.int32, (cells, cells), 0)
    qid = lax.broadcasted_iota(jnp.int32, (cells, cells), 1)
    mid = WIN * SHIFT
    row_diff = jnp.where((kid >= mid) != (qid >= mid), MASKED_SCORE, 0.0)
    kcol, qcol = lax.rem(kid, WIN) >= SHIFT, lax.rem(qid, WIN) >= SHIFT
    col_diff = jnp.where(kcol != qcol, MASKED_SCORE, 0.0)
    row_bias = row_diff * jnp.where(me_r == rows - 1, 1.0, 0.0)
    last_bias = row_bias + col_diff * jnp.where(me_c == cols - 1, 1.0, 0.0)

    for copy in halos[0:3]:
        copy.wait()
    lane = lax.broadcasted_iota(jnp.int32, (SHIFT, 2 * tile_cols), 1)
    dx[0:SHIFT, :] = jnp.where(lane < tile_cols, dom_out[SHIFT:, :], ext_d[1, SHIFT:, :])
    dx[SHIFT:, :] = jnp.where(lane < tile_cols, ext_d[0, 0:SHIFT, :], ext_d[2, 0:SHIFT, :])
    pick = lax.broadcasted_iota(jnp.int32, (WIN, 2 * tile_cols), 1) - lax.broadcasted_iota(
        jnp.int32, (WIN, 2 * tile_cols), 0
    )

    def attend(ws, t):
        at = slice(t * half, (t + 1) * half)
        k_at = slice(channels + t * half, channels + (t + 1) * half)
        v_at = slice(2 * channels + t * half, 2 * channels + (t + 1) * half)
        heads = (per, cells, cells)
        flat = (per * cells, cells)
        kx = [(proj[w, :, k_at][None] * hm).reshape(per * cells, half) for w in ws]
        vx = [(proj[w, :, v_at][None] * hm).reshape(per * cells, half) for w in ws]
        s = [nt(k, proj[w, :, at]).reshape(heads) for k, w in zip(kx, ws)]
        dp = [nt(v, dctx[w, :, at]).astype(BF16).astype(F32).reshape(heads) for v, w in zip(vx, ws)]
        s = [x + (last_bias if w == windows - 1 else row_bias)[None] for x, w in zip(s, ws)]
        e = [jnp.exp2((x - jnp.max(x, 1, keepdims=True)) * (scale * LOG2E)) for x in s]
        p = [x * (1.0 / jnp.sum(x, 1, keepdims=True)) for x in e]
        pb = [x.astype(BF16).reshape(flat) for x in p]
        ds = [x * (y - jnp.sum(x * y, 1, keepdims=True)) for x, y in zip(p, dp)]
        dsb = [x.astype(BF16).reshape(flat) for x in ds]
        for n, w in enumerate(ws):
            ctx[w, :, at] = tn(pb[n], vx[n]).astype(BF16)
        for n, w in enumerate(ws):
            dv = nn(pb[n], dctx[w, :, at]).reshape(per, cells, half) * hm32
            dproj[w, :, v_at] = jnp.sum(dv, 0).astype(BF16)
        for n, w in enumerate(ws):
            dproj[w, :, at] = (tn(dsb[n], kx[n]) * scale).astype(BF16)
        for n, w in enumerate(ws):
            dk = nn(dsb[n], proj[w, :, at]).reshape(per, cells, half) * hm32
            dproj[w, :, k_at] = (jnp.sum(dk, 0) * scale).astype(BF16)

    gsum = jnp.zeros((WIN, channels), F32)
    outs = []
    for b in range(chunks):
        halos[3 + b].wait()
        block = slice(cuts[b], cuts[b + 1])
        xf[SHIFT:, block, :] = ext[0, SHIFT:, block, :].astype(F32)
        cf[SHIFT:, block, :] = ext[1, SHIFT:, block, :].astype(F32)
        if b == chunks - 1:
            for copy in halos[3 + chunks :]:
                copy.wait()
            block = slice(tile_cols, tile_cols + PAD)
            xf[:, block, :] = ext[0, :, block, :].astype(F32)
            cf[:, block, :] = ext[1, :, block, :].astype(F32)
        mine_w = range(b * each, (b + 1) * each)
        for w in mine_w:
            for i in range(tile_rows):
                line = jnp.broadcast_to(dx[i : i + 1, :], (WIN, 2 * tile_cols))
                mask[w, i * WIN : (i + 1) * WIN, :] = jnp.sum(
                    jnp.where(pick == w * WIN + SHIFT, line, 0.0), -1, keepdims=True
                )
            at = slice(w * WIN + SHIFT, (w + 1) * WIN + SHIFT)
            x = xf[:, at, :].reshape(cells, channels)
            average = jnp.mean(x, -1, keepdims=True)
            centred = x - average
            variance = jnp.mean(centred * centred, -1, keepdims=True)
            inv = lax.rsqrt(variance + NORM_EPSILON)
            standard = centred * inv
            rstd[w] = inv
            xhat[w] = standard
            shifted[w] = (standard * gain).astype(BF16)
            c = cf[:, at, :].reshape(cells, channels)
            datt[w] = (c * mask[w]).astype(BF16)
        ws = slice(b * each, (b + 1) * each)
        count = each * cells
        s_chunk = shifted[ws].reshape(count, channels)
        d_chunk = datt[ws].reshape(count, channels)
        proj[ws] = nn(s_chunk, wqkv_ref[...]).astype(BF16).reshape(each, cells, 3 * channels)
        dctx[ws] = nt(d_chunk, wproj_ref[...]).astype(BF16).reshape(each, cells, channels)
        attend(mine_w, 0)

    total = windows * cells
    hrows = channels // 2
    share = hrows // INNER
    wide = 4 * half
    other = dev(me_r, c_right)

    def half_sum(core, t):
        at = pl.ds(pl.multiple_of(core * hrows, hrows), hrows)
        left_s = shifted[:, :, at].reshape(total, hrows)
        right_d = datt[:, :, at].reshape(total, hrows)
        heads = [
            dproj[:, :, n * channels + t * half : n * channels + (t + 1) * half].reshape(total, half)
            for n in range(3)
        ]
        left_c = ctx[:, :, t * half : (t + 1) * half].reshape(total, half)
        return tn(left_s, jnp.concatenate(heads, 1)), tn(left_c, right_d)

    def core_start(t):
        sum_q, sum_p = half_sum(c_right, t)
        core_out[t, :, 0 : 3 * half] = sum_q.astype(BF16)
        core_out[t, :, 3 * half :] = sum_p.astype(BF16)
        copy = remote(core_out.at[t], core_in.at[t], core_send.at[t], core_recv.at[t], other)
        copy.start()
        sum_q, sum_p = half_sum(me_c, t)
        own_part[t, :, 0 : 3 * half] = sum_q
        own_part[t, :, 3 * half :] = sum_p
        return copy

    def chip_sum(j, t):
        at = pl.ds(pl.multiple_of(j * share, share), share)
        sbuf[t, j, :, 0:wide] = (own_part[t, at, :] + core_in[t, at, :].astype(F32)).astype(BF16)

    def scatter_start(t):
        copies = [None]
        for o in range(1, INNER):
            j = lax.rem(member + o, INNER)
            chip_sum(j, t)
            copy = remote(
                sbuf.at[t, j],
                rbuf.at[t, o],
                rs_send.at[t, o],
                rs_recv.at[t, o],
                dev(peer(o), me_c),
            )
            copy.start()
            copies.append(copy)
        chip_sum(member, t)
        return copies

    def scatter_end(t, copies):
        acc = sbuf[t, member].astype(F32)
        for o in range(1, INNER):
            copies[o].wait()
            acc = acc + rbuf[t, o].astype(F32)
        return acc

    def gather_start(t, acc, extra):
        acc = jnp.concatenate([acc, extra], 1)
        if outer > 1:
            obuf[t] = acc.astype(BF16)
            spread = [
                remote(
                    obuf.at[t],
                    oin.at[t, o],
                    o_send.at[t, o],
                    o_recv.at[t, o],
                    dev(counterpart(o), me_c),
                )
                for o in range(1, outer)
            ]
            for copy in spread:
                copy.start()
            for o in range(1, outer):
                spread[o - 1].wait()
                acc = acc + oin[t, o].astype(F32)
        mine = gsum_ref.at[t, me_c, member]
        mine[...] = acc.astype(BF16)
        copies = [
            remote(mine, mine, ag_send.at[t, o], ag_recv.at[t, o], dev(peer(o), me_c))
            for o in range(1, INNER)
        ]
        for copy in copies:
            copy.start()
        return copies

    def gather_end(t, copies):
        for copy in copies:
            copy.wait()
        column = gsum_ref.at[t, me_c]
        copy = remote(column, column, fw_send.at[t], fw_recv.at[t], other)
        copy.start()
        return copy

    early = core_start(0)
    for b in range(chunks):
        ws = slice(b * each, (b + 1) * each)
        mine_w = range(b * each, (b + 1) * each)
        attend(mine_w, 1)
        if b == 0:
            early.wait()
            early_scatter = scatter_start(0)
        if b == chunks - 1:
            acc = scatter_end(0, early_scatter)
            early_gather = gather_start(0, acc, jnp.zeros((share, 128), F32))
            late = core_start(1)
        p_chunk = dproj[ws].reshape(count, 3 * channels)
        dnormed = nt(p_chunk, wqkv_ref[...]).astype(BF16).astype(F32)
        c_chunk = ctx[ws].reshape(count, channels)
        attended = nn(c_chunk, wproj_ref[...]).astype(BF16).astype(F32)
        for u, w in enumerate(mine_w):
            at = slice(w * WIN + SHIFT, (w + 1) * WIN + SHIFT)
            dn = dnormed[u * cells : (u + 1) * cells]
            standard = xhat[w]
            gsum = gsum + jnp.sum((dn * standard).reshape(WIN, WIN, channels), 0)
            up_grad = dn * gain
            mean_g = jnp.mean(up_grad, -1, keepdims=True)
            mean_gx = jnp.mean(up_grad * standard, -1, keepdims=True)
            grad = rstd[w] * (up_grad - mean_g - standard * mean_gx)
            out32[1, :, at, :] = cf[:, at, :] + grad.reshape(WIN, WIN, channels)
            inside = mask[w] * attended[u * cells : (u + 1) * cells]
            out32[0, :, at, :] = xf[:, at, :] + inside.reshape(WIN, WIN, channels)
        block = slice(b * reach * PAD, (b + 1) * reach * PAD)
        outx[:, :, block, :] = out32[:, :, block, :].astype(BF16)
        area = pl.ds(b * reach * PAD, reach * PAD)
        copy = remote(
            outx.at[both, low, area],
            row_in.at[both, top, area],
            out_send.at[b],
            out_recv.at[b],
            dev(r_dn, me_c),
        )
        copy.start()
        outs.append(copy)

    late.wait()
    late_scatter = scatter_start(1)
    gtile = jnp.concatenate([gsum[:, :half], gsum[:, half:]], 0)
    gcore_out[...] = gtile.astype(BF16)
    gain_copy = remote(gcore_out, gcore_in, core_send.at[2], core_recv.at[2], other)
    gain_copy.start()
    edge = slice(tile_cols, tile_cols + PAD)
    outx[:, :, edge, :] = out32[:, :, edge, :].astype(BF16)
    last = [
        remote(
            outx.at[both, top, side],
            col_in,
            out_send.at[blocks],
            out_recv.at[blocks],
            dev(me_r, c_right),
        ),
        remote(
            outx.at[both, low, side],
            diag_in,
            out_send.at[blocks + 1],
            out_recv.at[blocks + 1],
            dev(r_dn, c_right),
        ),
    ]
    for copy in last:
        copy.start()
    outs += last
    early_hand = gather_end(0, early_gather)
    gain_copy.wait()
    gchip = gtile + gcore_in[...].astype(F32)
    late_gather = gather_start(1, scatter_end(1, late_scatter), gchip)

    def give(i, src, dst):
        copy = pltpu.make_async_copy(src, dst, done_sem.at[i])
        copy.start()
        return copy

    results = []
    for copy in outs:
        copy.wait()
    col_id = lax.broadcasted_iota(jnp.int32, (SHIFT, PAD, channels), 1)
    for n, ref in enumerate((upd_ref, gfeat_ref)):
        ref[0:SHIFT, PAD:, :] = row_in[n, :, PAD:, :]
        ref[SHIFT:, PAD:, :] = outx[n, 0:SHIFT, PAD:tile_cols, :]
        ref[0:SHIFT, 0:PAD, :] = jnp.where(
            col_id < SHIFT, diag_in[n].astype(F32), row_in[n, :, 0:PAD, :].astype(F32)
        ).astype(BF16)
        ref[SHIFT:, 0:PAD, :] = jnp.where(
            col_id < SHIFT, col_in[n].astype(F32), outx[n, 0:SHIFT, 0:PAD, :].astype(F32)
        ).astype(BF16)
    results += [give(1, upd_ref, upd_hbm), give(2, gfeat_ref, gfeat_hbm)]

    late_hand = gather_end(1, late_gather)
    results.append(give(3, gsum_ref.at[both, me_c], gsum_hbm.at[both, me_c]))
    gains = jnp.sum(gsum_ref[1, me_c, :, :, wide:].astype(F32), 0)
    gfold = jnp.concatenate([gains[0:WIN], gains[WIN:]], 1)
    ggain_ref[...] = jnp.sum(gfold, 0, keepdims=True)
    results.append(give(0, ggain_ref, ggain_hbm))
    early_hand.wait()
    late_hand.wait()
    results.append(give(4, gsum_ref.at[both, c_right], gsum_hbm.at[both, c_right]))
    for copy in results:
        copy.wait()


def finish(
    upd_in,
    gfeat_in,
    gsum_in,
    ggain_in,
    upd,
    gfeat,
    gqkv,
    gproj,
    ggain,
    upd_mid,
    gfeat_mid,
    ggain_mid,
    sums,
    qkv32,
    proj32,
    in_sems,
    out_sems,
):
    channels = gqkv.shape[0]
    parts, halves, _, _, wide = sums.shape
    hrows = channels // halves
    half = 128
    pairs = [(t, c) for t in range(parts) for c in range(halves)]

    def copies(jobs, sems):
        return [pltpu.make_async_copy(s, d, sems.at[i]) for i, (s, d) in enumerate(jobs)]

    reads = [(gsum_in.at[t, c], sums.at[t, c]) for t, c in pairs]
    reads += [(upd_in, upd_mid), (gfeat_in, gfeat_mid), (ggain_in, ggain_mid)]
    writes = [(qkv32, gqkv), (proj32, gproj)]
    writes += [(upd_mid, upd), (gfeat_mid, gfeat), (ggain_mid, ggain)]
    reads, writes = copies(reads, in_sems), copies(writes, out_sems)
    for copy in reads:
        copy.start()
    for n, (t, c) in enumerate(pairs):
        reads[n].wait()
        some = sums[t, c].reshape(hrows, wide).astype(F32)
        rows = slice(c * hrows, (c + 1) * hrows)
        for n in range(3):
            at = slice(n * channels + t * half, n * channels + (t + 1) * half)
            qkv32[rows, at] = some[:, n * half : (n + 1) * half]
        proj32[t * half : (t + 1) * half, rows] = some[:, 3 * half : 4 * half]
    for n in range(2):
        writes[n].start()
    for n in range(3):
        reads[len(pairs) + n].wait()
        writes[2 + n].start()
    for copy in writes:
        copy.wait()


def on_device(features, cotangent, domain, qkv_weight, proj_weight, norm_gain):
    tile_rows, tile_cols, channels = features.shape
    rows, cols = lax.axis_size("row"), lax.axis_size("col")
    outer = rows // INNER
    windows, cells = tile_cols // WIN, WIN * WIN
    blocks = tile_cols // PAD
    piece = channels // 2 // INNER
    wide = 4 * 128
    ext = tile_cols + PAD
    vm = pltpu.VMEM
    dma = pltpu.SemaphoreType.DMA
    halos = 3 + blocks + 2
    aspec = pl.BlockSpec(memory_space=pltpu.HBM)
    results = pl.pallas_call(
        functools.partial(kernel, rows, cols),
        out_shape=(
            jax.ShapeDtypeStruct(features.shape, BF16),
            jax.ShapeDtypeStruct(features.shape, BF16),
            jax.ShapeDtypeStruct((2, 2, INNER, piece, wide + 128), BF16),
            jax.ShapeDtypeStruct((1, channels), F32),
        ),
        in_specs=[aspec] * 6,
        out_specs=(aspec,) * 4,
        scratch_shapes=[
            vm(features.shape, BF16),
            vm(features.shape, BF16),
            vm((2, 2, INNER, piece, wide + 128), BF16),
            vm((1, channels), F32),
            vm(qkv_weight.shape, BF16),
            vm(proj_weight.shape, BF16),
            vm((1, channels), F32),
            vm((tile_rows, tile_cols), jnp.int32),
            vm((tile_rows, 2 * tile_cols), F32),
            vm((2, tile_rows, tile_cols, channels), BF16),
            vm((2, tile_rows, ext, channels), BF16),
            vm((3, tile_rows, 2 * tile_cols), F32),
            vm((tile_rows, ext, channels), F32),
            vm((tile_rows, ext, channels), F32),
            vm((tile_rows, 2 * tile_cols), F32),
            vm((windows, cells, 1), F32),
            vm((windows, cells, channels), F32),
            vm((windows, cells, 1), F32),
            vm((windows, cells, channels), BF16),
            vm((windows, cells, channels), BF16),
            vm((windows, cells, 3 * channels), BF16),
            vm((windows, cells, 3 * channels), BF16),
            vm((windows, cells, channels), BF16),
            vm((windows, cells, channels), BF16),
            vm((2, tile_rows, ext, channels), F32),
            vm((2, tile_rows, ext, channels), BF16),
            vm((2, SHIFT, tile_cols, channels), BF16),
            vm((2, SHIFT, PAD, channels), BF16),
            vm((2, SHIFT, PAD, channels), BF16),
            vm((2, channels // 2, wide), F32),
            vm((2, channels // 2, wide), BF16),
            vm((2, channels // 2, wide), BF16),
            vm((16, 128), BF16),
            vm((16, 128), BF16),
            vm((2, INNER, piece, wide), BF16),
            vm((2, INNER, piece, wide), BF16),
            vm((2, piece, wide + 128), BF16),
            vm((2, outer, piece, wide + 128), BF16),
            dma((6,)),
            dma((5,)),
            dma((halos,)),
            dma((halos,)),
            dma((blocks + 2,)),
            dma((blocks + 2,)),
            dma((3,)),
            dma((3,)),
            dma((2, INNER)),
            dma((2, INNER)),
            dma((2, outer)),
            dma((2, outer)),
            dma((2, INNER)),
            dma((2, INNER)),
            dma((2,)),
            dma((2,)),
        ],
        compiler_params=pltpu.CompilerParams(
            collective_id=0, has_side_effects=True, vmem_limit_bytes=60 * 1024 * 1024
        ),
    )(features, cotangent, domain, qkv_weight, proj_weight, norm_gain[None, :])
    outs = pl.pallas_call(
        finish,
        out_shape=(
            jax.ShapeDtypeStruct(features.shape, BF16),
            jax.ShapeDtypeStruct(features.shape, BF16),
            jax.ShapeDtypeStruct((channels, 3 * channels), F32),
            jax.ShapeDtypeStruct((channels, channels), F32),
            jax.ShapeDtypeStruct((1, channels), F32),
        ),
        in_specs=[aspec] * 4,
        out_specs=(aspec,) * 5,
        scratch_shapes=[
            vm(features.shape, BF16),
            vm(features.shape, BF16),
            vm((1, channels), F32),
            vm((2, 2, INNER, piece, wide + 128), BF16),
            vm((channels, 3 * channels), F32),
            vm((channels, channels), F32),
            dma((7,)),
            dma((5,)),
        ],
        compiler_params=pltpu.CompilerParams(vmem_limit_bytes=60 * 1024 * 1024),
    )(*results)
    return (outs[0], outs[1], outs[2], outs[3], outs[4].reshape(channels))


def solution(mesh):
    return jax.shard_map(
        on_device,
        mesh=mesh,
        in_specs=(
            P(("grp", "row"), "col", None),
            P(("grp", "row"), "col", None),
            P(("grp", "row"), "col"),
            P(),
            P(),
            P(),
        ),
        out_specs=(
            P(("grp", "row"), "col", None),
            P(("grp", "row"), "col", None),
            P("grp", None),
            P("grp", None),
            P("grp"),
        ),
        check_vma=False,
    )
```

```python
import functools

import jax
import jax.numpy as jnp
from jax import lax
from jax.experimental import pallas as pl
from jax.experimental.pallas import tpu as pltpu
from jax.sharding import PartitionSpec as P

HEADS = 8
WIN = 8
SHIFT = 4
NORM_EPSILON = 1e-05
MASKED_SCORE = -1e30
LOG2E = 1.4426950408889634
INNER = 8
PAD = 16

F32 = jnp.float32
BF16 = jnp.bfloat16


def nn(a, b):
    return lax.dot_general(a, b, (((1,), (0,)), ((), ())), preferred_element_type=F32)


def nt(a, b):
    return lax.dot_general(a, b, (((1,), (1,)), ((), ())), preferred_element_type=F32)


def tn(a, b):
    return lax.dot_general(a, b, (((0,), (0,)), ((), ())), preferred_element_type=F32)


def kernel(
    rows,
    cols,
    feat_hbm,
    cot_hbm,
    dom_hbm,
    wqkv_hbm,
    wproj_hbm,
    gain_hbm,
    upd_hbm,
    gfeat_hbm,
    gsum_hbm,
    ggain_hbm,
    upd_ref,
    gfeat_ref,
    gsum_ref,
    ggain_ref,
    wqkv_ref,
    wproj_ref,
    gain_ref,
    dom_ref,
    dom_out,
    own,
    ext,
    ext_d,
    xf,
    cf,
    dx,
    mask,
    xhat,
    rstd,
    shifted,
    datt,
    proj,
    dproj,
    ctx,
    dctx,
    out32,
    outx,
    row_in,
    col_in,
    own_part,
    core_out,
    core_in,
    gcore_out,
    gcore_in,
    sbuf,
    rbuf,
    obuf,
    oin,
    local_sem,
    done_sem,
    in_send,
    in_recv,
    out_send,
    out_recv,
    core_send,
    core_recv,
    rs_send,
    rs_recv,
    o_send,
    o_recv,
    ag_send,
    ag_recv,
    fw_send,
    fw_recv,
):
    tile_rows, tile_cols, channels = feat_hbm.shape
    windows = tile_cols // WIN
    cells = WIN * WIN
    head_dim = channels // HEADS
    blocks = tile_cols // PAD
    chunks = 4
    each = windows // chunks
    reach = blocks // chunks
    outer = rows // INNER
    me_r = lax.axis_index("row")
    me_c = lax.axis_index("col")
    r_up = lax.rem(me_r + rows - 1, rows)
    r_dn = lax.rem(me_r + 1, rows)
    c_left = lax.rem(me_c + cols - 1, cols)
    c_right = lax.rem(me_c + 1, cols)
    group = me_r // INNER
    member = lax.rem(me_r, INNER)

    def dev(r, c):
        return {"row": r, "col": c}

    def peer(o):
        return group * INNER + lax.rem(member + o, INNER)

    def counterpart(o):
        return lax.rem(group + o, outer) * INNER + member

    barrier = pltpu.get_barrier_semaphore()
    greeted = [
        dev(r_up, me_c),
        dev(r_dn, me_c),
        dev(me_r, c_left),
        dev(r_up, c_left),
        dev(r_dn, c_right),
    ]
    greeted += [dev(peer(o), me_c) for o in range(1, INNER)]
    greeted += [dev(counterpart(o), me_c) for o in range(1, outer)]
    for target in greeted:
        pl.semaphore_signal(barrier, inc=1, device_id=target, device_id_type=pl.DeviceIdType.MESH)

    top, low = pl.ds(0, SHIFT), pl.ds(SHIFT, SHIFT)
    body, side, head = pl.ds(0, tile_cols), pl.ds(tile_cols, PAD), pl.ds(0, PAD)
    local = [
        pltpu.make_async_copy(s, d, local_sem.at[i])
        for i, (s, d) in enumerate(
            (
                (dom_hbm, dom_ref),
                (feat_hbm, own.at[0]),
                (cot_hbm, own.at[1]),
                (gain_hbm, gain_ref),
                (wqkv_hbm, wqkv_ref),
                (wproj_hbm, wproj_ref),
            )
        )
    ]
    for copy in local:
        copy.start()
    out32[:, :, 0:8, :] = jnp.zeros((2, tile_rows, 8, channels), F32)
    out32[:, :, tile_cols : tile_cols + PAD, :] = jnp.zeros((2, tile_rows, PAD, channels), F32)
    local[0].wait()
    dom = dom_ref[...].astype(F32)
    dom_out[...] = jnp.concatenate([dom, dom], 1)
    for copy in local[1:3]:
        copy.wait()
    pl.semaphore_wait(barrier, len(greeted))

    def remote(src, dst, send, recv, target):
        return pltpu.make_async_remote_copy(
            src_ref=src,
            dst_ref=dst,
            send_sem=send,
            recv_sem=recv,
            device_id=target,
            device_id_type=pl.DeviceIdType.MESH,
        )

    up, left, corner = dev(r_up, me_c), dev(me_r, c_left), dev(r_up, c_left)
    both = pl.ds(0, 2)
    jobs = [(dom_out, ext_d.at[i], t) for i, t in enumerate((up, left, corner))]
    cuts = [0] + [(b * reach + 1) * PAD for b in range(1, chunks)] + [tile_cols]
    for first, end in zip(cuts, cuts[1:]):
        if first < end:
            area = pl.ds(first, end - first)
            jobs.append((own.at[both, top, area], ext.at[both, low, area], up))
    jobs.append((own.at[both, low, head], ext.at[both, top, side], left))
    halos = [
        remote(s, d, in_send.at[i], in_recv.at[i], t) for i, (s, d, t) in enumerate(jobs)
    ]
    for copy in halos:
        copy.start()
    xf[0:SHIFT, 0:tile_cols, :] = own[0, SHIFT:, :, :].astype(F32)
    cf[0:SHIFT, 0:tile_cols, :] = own[1, SHIFT:, :, :].astype(F32)
    for copy in local[3:]:
        copy.wait()
    gain = gain_ref[...]

    scale = head_dim ** (-0.5)
    half = 128
    per = half // head_dim
    hid = lax.broadcasted_iota(jnp.int32, (per, 1, half), 0)
    lid = lax.broadcasted_iota(jnp.int32, (per, 1, half), 2) // head_dim
    hm32 = jnp.where(hid == lid, 1.0, 0.0).astype(F32)
    hm = hm32.astype(BF16)
    kid = lax.broadcasted_iota(jnp.int32, (cells, cells), 0)
    qid = lax.broadcasted_iota(jnp.int32, (cells, cells), 1)
    mid = WIN * SHIFT
    row_diff = jnp.where((kid >= mid) != (qid >= mid), MASKED_SCORE, 0.0)
    kcol, qcol = lax.rem(kid, WIN) >= SHIFT, lax.rem(qid, WIN) >= SHIFT
    col_diff = jnp.where(kcol != qcol, MASKED_SCORE, 0.0)
    row_bias = row_diff * jnp.where(me_r == rows - 1, 1.0, 0.0)
    last_bias = row_bias + col_diff * jnp.where(me_c == cols - 1, 1.0, 0.0)

    for copy in halos[0:3]:
        copy.wait()
    lane = lax.broadcasted_iota(jnp.int32, (SHIFT, 2 * tile_cols), 1)
    dx[0:SHIFT, :] = jnp.where(lane < tile_cols, dom_out[SHIFT:, :], ext_d[1, SHIFT:, :])
    dx[SHIFT:, :] = jnp.where(lane < tile_cols, ext_d[0, 0:SHIFT, :], ext_d[2, 0:SHIFT, :])
    pick = lax.broadcasted_iota(jnp.int32, (WIN, 2 * tile_cols), 1) - lax.broadcasted_iota(
        jnp.int32, (WIN, 2 * tile_cols), 0
    )

    def attend(ws, t):
        at = slice(t * half, (t + 1) * half)
        k_at = slice(channels + t * half, channels + (t + 1) * half)
        v_at = slice(2 * channels + t * half, 2 * channels + (t + 1) * half)
        heads = (per, cells, cells)
        flat = (per * cells, cells)
        kx = [(proj[w, :, k_at][None] * hm).reshape(per * cells, half) for w in ws]
        vx = [(proj[w, :, v_at][None] * hm).reshape(per * cells, half) for w in ws]
        s = [nt(k, proj[w, :, at]).reshape(heads) for k, w in zip(kx, ws)]
        dp = [nt(v, dctx[w, :, at]).astype(BF16).astype(F32).reshape(heads) for v, w in zip(vx, ws)]
        s = [x + (last_bias if w == windows - 1 else row_bias)[None] for x, w in zip(s, ws)]
        e = [jnp.exp2((x - jnp.max(x, 1, keepdims=True)) * (scale * LOG2E)) for x in s]
        p = [x * (1.0 / jnp.sum(x, 1, keepdims=True)) for x in e]
        pb = [x.astype(BF16).reshape(flat) for x in p]
        ds = [x * (y - jnp.sum(x * y, 1, keepdims=True)) for x, y in zip(p, dp)]
        dsb = [x.astype(BF16).reshape(flat) for x in ds]
        for n, w in enumerate(ws):
            ctx[w, :, at] = tn(pb[n], vx[n]).astype(BF16)
        for n, w in enumerate(ws):
            dv = nn(pb[n], dctx[w, :, at]).reshape(per, cells, half) * hm32
            dproj[w, :, v_at] = jnp.sum(dv, 0).astype(BF16)
        for n, w in enumerate(ws):
            dproj[w, :, at] = (tn(dsb[n], kx[n]) * scale).astype(BF16)
        for n, w in enumerate(ws):
            dk = nn(dsb[n], proj[w, :, at]).reshape(per, cells, half) * hm32
            dproj[w, :, k_at] = (jnp.sum(dk, 0) * scale).astype(BF16)

    gsum = jnp.zeros((WIN, channels), F32)
    outs = []
    for b in range(chunks):
        if cuts[b] < cuts[b + 1]:
            halos[3 + b].wait()
            block = slice(cuts[b], cuts[b + 1])
            xf[SHIFT:, block, :] = ext[0, SHIFT:, block, :].astype(F32)
            cf[SHIFT:, block, :] = ext[1, SHIFT:, block, :].astype(F32)
        if b == 0:
            at = len(jobs)
            passed = remote(
                ext.at[both, low, head], ext.at[both, low, side], in_send.at[at], in_recv.at[at], left
            )
            passed.start()
        if b == chunks - 1:
            halos[-1].wait()
            passed.wait()
            block = slice(tile_cols, tile_cols + PAD)
            xf[:, block, :] = ext[0, :, block, :].astype(F32)
            cf[:, block, :] = ext[1, :, block, :].astype(F32)
        mine_w = range(b * each, (b + 1) * each)
        for w in mine_w:
            for i in range(tile_rows):
                line = jnp.broadcast_to(dx[i : i + 1, :], (WIN, 2 * tile_cols))
                mask[w, i * WIN : (i + 1) * WIN, :] = jnp.sum(
                    jnp.where(pick == w * WIN + SHIFT, line, 0.0), -1, keepdims=True
                )
            at = slice(w * WIN + SHIFT, (w + 1) * WIN + SHIFT)
            x = xf[:, at, :].reshape(cells, channels)
            average = jnp.mean(x, -1, keepdims=True)
            centred = x - average
            variance = jnp.mean(centred * centred, -1, keepdims=True)
            inv = lax.rsqrt(variance + NORM_EPSILON)
            standard = centred * inv
            rstd[w] = inv
            xhat[w] = standard
            shifted[w] = (standard * gain).astype(BF16)
            c = cf[:, at, :].reshape(cells, channels)
            datt[w] = (c * mask[w]).astype(BF16)
        ws = slice(b * each, (b + 1) * each)
        count = each * cells
        s_chunk = shifted[ws].reshape(count, channels)
        d_chunk = datt[ws].reshape(count, channels)
        proj[ws] = nn(s_chunk, wqkv_ref[...]).astype(BF16).reshape(each, cells, 3 * channels)
        dctx[ws] = nt(d_chunk, wproj_ref[...]).astype(BF16).reshape(each, cells, channels)
        attend(mine_w, 0)

    total = windows * cells
    hrows = channels // 2
    share = hrows // INNER
    wide = 4 * half
    other = dev(me_r, c_right)

    def half_sum(core, t):
        at = pl.ds(pl.multiple_of(core * hrows, hrows), hrows)
        left_s = shifted[:, :, at].reshape(total, hrows)
        right_d = datt[:, :, at].reshape(total, hrows)
        heads = [
            dproj[:, :, n * channels + t * half : n * channels + (t + 1) * half].reshape(total, half)
            for n in range(3)
        ]
        left_c = ctx[:, :, t * half : (t + 1) * half].reshape(total, half)
        return tn(left_s, jnp.concatenate(heads, 1)), tn(left_c, right_d)

    def core_start(t):
        sum_q, sum_p = half_sum(c_right, t)
        core_out[t, :, 0 : 3 * half] = sum_q.astype(BF16)
        core_out[t, :, 3 * half :] = sum_p.astype(BF16)
        copy = remote(core_out.at[t], core_in.at[t], core_send.at[t], core_recv.at[t], other)
        copy.start()
        sum_q, sum_p = half_sum(me_c, t)
        own_part[t, :, 0 : 3 * half] = sum_q
        own_part[t, :, 3 * half :] = sum_p
        return copy

    def chip_sum(j, t):
        at = pl.ds(pl.multiple_of(j * share, share), share)
        sbuf[t, j, :, 0:wide] = (own_part[t, at, :] + core_in[t, at, :].astype(F32)).astype(BF16)

    def scatter_start(t):
        copies = [None]
        for o in range(1, INNER):
            j = lax.rem(member + o, INNER)
            chip_sum(j, t)
            copy = remote(
                sbuf.at[t, j],
                rbuf.at[t, o],
                rs_send.at[t, o],
                rs_recv.at[t, o],
                dev(peer(o), me_c),
            )
            copy.start()
            copies.append(copy)
        chip_sum(member, t)
        return copies

    def scatter_end(t, copies):
        acc = sbuf[t, member].astype(F32)
        for o in range(1, INNER):
            copies[o].wait()
            acc = acc + rbuf[t, o].astype(F32)
        return acc

    def gather_start(t, acc, extra):
        acc = jnp.concatenate([acc, extra], 1)
        if outer > 1:
            obuf[t] = acc.astype(BF16)
            spread = [
                remote(
                    obuf.at[t],
                    oin.at[t, o],
                    o_send.at[t, o],
                    o_recv.at[t, o],
                    dev(counterpart(o), me_c),
                )
                for o in range(1, outer)
            ]
            for copy in spread:
                copy.start()
            for o in range(1, outer):
                spread[o - 1].wait()
                acc = acc + oin[t, o].astype(F32)
        mine = gsum_ref.at[t, me_c, member]
        mine[...] = acc.astype(BF16)
        copies = [
            remote(mine, mine, ag_send.at[t, o], ag_recv.at[t, o], dev(peer(o), me_c))
            for o in range(1, INNER)
        ]
        for copy in copies:
            copy.start()
        return copies

    def gather_end(t, copies):
        for copy in copies:
            copy.wait()
        column = gsum_ref.at[t, me_c]
        copy = remote(column, column, fw_send.at[t], fw_recv.at[t], other)
        copy.start()
        return copy

    early = core_start(0)
    for b in range(chunks):
        ws = slice(b * each, (b + 1) * each)
        mine_w = range(b * each, (b + 1) * each)
        attend(mine_w, 1)
        if b == 0:
            early.wait()
            early_scatter = scatter_start(0)
        if b == chunks - 1:
            acc = scatter_end(0, early_scatter)
            early_gather = gather_start(0, acc, jnp.zeros((share, 128), F32))
            late = core_start(1)
        p_chunk = dproj[ws].reshape(count, 3 * channels)
        dnormed = nt(p_chunk, wqkv_ref[...]).astype(BF16).astype(F32)
        c_chunk = ctx[ws].reshape(count, channels)
        attended = nn(c_chunk, wproj_ref[...]).astype(BF16).astype(F32)
        for u, w in enumerate(mine_w):
            at = slice(w * WIN + SHIFT, (w + 1) * WIN + SHIFT)
            dn = dnormed[u * cells : (u + 1) * cells]
            standard = xhat[w]
            gsum = gsum + jnp.sum((dn * standard).reshape(WIN, WIN, channels), 0)
            up_grad = dn * gain
            mean_g = jnp.mean(up_grad, -1, keepdims=True)
            mean_gx = jnp.mean(up_grad * standard, -1, keepdims=True)
            grad = rstd[w] * (up_grad - mean_g - standard * mean_gx)
            out32[1, :, at, :] = cf[:, at, :] + grad.reshape(WIN, WIN, channels)
            inside = mask[w] * attended[u * cells : (u + 1) * cells]
            out32[0, :, at, :] = xf[:, at, :] + inside.reshape(WIN, WIN, channels)
        block = slice(b * reach * PAD, (b + 1) * reach * PAD)
        outx[:, :, block, :] = out32[:, :, block, :].astype(BF16)
        first = max(b * reach, 1) * PAD
        area = pl.ds(first, (b + 1) * reach * PAD - first)
        if first < (b + 1) * reach * PAD:
            copy = remote(
                outx.at[both, low, area],
                row_in.at[both, top, area],
                out_send.at[b],
                out_recv.at[b],
                dev(r_dn, me_c),
            )
            copy.start()
            outs.append(copy)

    edge = slice(tile_cols, tile_cols + PAD)
    outx[:, :, edge, :] = out32[:, :, edge, :].astype(BF16)
    aside = remote(
        outx.at[both, pl.ds(0, tile_rows), side],
        col_in,
        out_send.at[blocks],
        out_recv.at[blocks],
        dev(me_r, c_right),
    )
    aside.start()
    late.wait()
    late_scatter = scatter_start(1)
    gtile = jnp.concatenate([gsum[:, :half], gsum[:, half:]], 0)
    gcore_out[...] = gtile.astype(BF16)
    gain_copy = remote(gcore_out, gcore_in, core_send.at[2], core_recv.at[2], other)
    gain_copy.start()
    aside.wait()
    col_id = lax.broadcasted_iota(jnp.int32, (tile_rows, PAD, channels), 1)
    for n in range(2):
        outx[n, :, 0:PAD, :] = jnp.where(
            col_id < SHIFT, col_in[n].astype(F32), outx[n, :, 0:PAD, :].astype(F32)
        ).astype(BF16)
    copy = remote(
        outx.at[both, low, head],
        row_in.at[both, top, head],
        out_send.at[blocks + 1],
        out_recv.at[blocks + 1],
        dev(r_dn, me_c),
    )
    copy.start()
    outs.append(copy)
    early_hand = gather_end(0, early_gather)
    gain_copy.wait()
    gchip = gtile + gcore_in[...].astype(F32)
    late_gather = gather_start(1, scatter_end(1, late_scatter), gchip)

    def give(i, src, dst):
        copy = pltpu.make_async_copy(src, dst, done_sem.at[i])
        copy.start()
        return copy

    results = []
    for copy in outs:
        copy.wait()
    for n, ref in enumerate((upd_ref, gfeat_ref)):
        ref[0:SHIFT, :, :] = row_in[n]
        ref[SHIFT:, :, :] = outx[n, 0:SHIFT, 0:tile_cols, :]
    results += [give(1, upd_ref, upd_hbm), give(2, gfeat_ref, gfeat_hbm)]

    late_hand = gather_end(1, late_gather)
    results.append(give(3, gsum_ref.at[both, me_c], gsum_hbm.at[both, me_c]))
    gains = jnp.sum(gsum_ref[1, me_c, :, :, wide:].astype(F32), 0)
    gfold = jnp.concatenate([gains[0:WIN], gains[WIN:]], 1)
    ggain_ref[...] = jnp.sum(gfold, 0, keepdims=True)
    results.append(give(0, ggain_ref, ggain_hbm))
    early_hand.wait()
    late_hand.wait()
    results.append(give(4, gsum_ref.at[both, c_right], gsum_hbm.at[both, c_right]))
    for copy in results:
        copy.wait()


def finish(
    upd_in,
    gfeat_in,
    gsum_in,
    ggain_in,
    upd,
    gfeat,
    gqkv,
    gproj,
    ggain,
    upd_mid,
    gfeat_mid,
    ggain_mid,
    sums,
    qkv32,
    proj32,
    in_sems,
    out_sems,
):
    channels = gqkv.shape[0]
    parts, halves, _, _, wide = sums.shape
    hrows = channels // halves
    half = 128
    pairs = [(t, c) for t in range(parts) for c in range(halves)]

    def copies(jobs, sems):
        return [pltpu.make_async_copy(s, d, sems.at[i]) for i, (s, d) in enumerate(jobs)]

    reads = [(gsum_in.at[t, c], sums.at[t, c]) for t, c in pairs]
    reads += [(upd_in, upd_mid), (gfeat_in, gfeat_mid), (ggain_in, ggain_mid)]
    writes = [(qkv32, gqkv), (proj32, gproj)]
    writes += [(upd_mid, upd), (gfeat_mid, gfeat), (ggain_mid, ggain)]
    reads, writes = copies(reads, in_sems), copies(writes, out_sems)
    for copy in reads:
        copy.start()
    for n, (t, c) in enumerate(pairs):
        reads[n].wait()
        some = sums[t, c].reshape(hrows, wide).astype(F32)
        rows = slice(c * hrows, (c + 1) * hrows)
        for n in range(3):
            at = slice(n * channels + t * half, n * channels + (t + 1) * half)
            qkv32[rows, at] = some[:, n * half : (n + 1) * half]
        proj32[t * half : (t + 1) * half, rows] = some[:, 3 * half : 4 * half]
    for n in range(2):
        writes[n].start()
    for n in range(3):
        reads[len(pairs) + n].wait()
        writes[2 + n].start()
    for copy in writes:
        copy.wait()


def on_device(features, cotangent, domain, qkv_weight, proj_weight, norm_gain):
    tile_rows, tile_cols, channels = features.shape
    rows, cols = lax.axis_size("row"), lax.axis_size("col")
    outer = rows // INNER
    windows, cells = tile_cols // WIN, WIN * WIN
    blocks = tile_cols // PAD
    piece = channels // 2 // INNER
    wide = 4 * 128
    ext = tile_cols + PAD
    vm = pltpu.VMEM
    dma = pltpu.SemaphoreType.DMA
    halos = 3 + blocks + 2
    aspec = pl.BlockSpec(memory_space=pltpu.HBM)
    results = pl.pallas_call(
        functools.partial(kernel, rows, cols),
        out_shape=(
            jax.ShapeDtypeStruct(features.shape, BF16),
            jax.ShapeDtypeStruct(features.shape, BF16),
            jax.ShapeDtypeStruct((2, 2, INNER, piece, wide + 128), BF16),
            jax.ShapeDtypeStruct((1, channels), F32),
        ),
        in_specs=[aspec] * 6,
        out_specs=(aspec,) * 4,
        scratch_shapes=[
            vm(features.shape, BF16),
            vm(features.shape, BF16),
            vm((2, 2, INNER, piece, wide + 128), BF16),
            vm((1, channels), F32),
            vm(qkv_weight.shape, BF16),
            vm(proj_weight.shape, BF16),
            vm((1, channels), F32),
            vm((tile_rows, tile_cols), jnp.int32),
            vm((tile_rows, 2 * tile_cols), F32),
            vm((2, tile_rows, tile_cols, channels), BF16),
            vm((2, tile_rows, ext, channels), BF16),
            vm((3, tile_rows, 2 * tile_cols), F32),
            vm((tile_rows, ext, channels), F32),
            vm((tile_rows, ext, channels), F32),
            vm((tile_rows, 2 * tile_cols), F32),
            vm((windows, cells, 1), F32),
            vm((windows, cells, channels), F32),
            vm((windows, cells, 1), F32),
            vm((windows, cells, channels), BF16),
            vm((windows, cells, channels), BF16),
            vm((windows, cells, 3 * channels), BF16),
            vm((windows, cells, 3 * channels), BF16),
            vm((windows, cells, channels), BF16),
            vm((windows, cells, channels), BF16),
            vm((2, tile_rows, ext, channels), F32),
            vm((2, tile_rows, ext, channels), BF16),
            vm((2, SHIFT, tile_cols, channels), BF16),
            vm((2, tile_rows, PAD, channels), BF16),
            vm((2, channels // 2, wide), F32),
            vm((2, channels // 2, wide), BF16),
            vm((2, channels // 2, wide), BF16),
            vm((16, 128), BF16),
            vm((16, 128), BF16),
            vm((2, INNER, piece, wide), BF16),
            vm((2, INNER, piece, wide), BF16),
            vm((2, piece, wide + 128), BF16),
            vm((2, outer, piece, wide + 128), BF16),
            dma((6,)),
            dma((5,)),
            dma((halos,)),
            dma((halos,)),
            dma((blocks + 2,)),
            dma((blocks + 2,)),
            dma((3,)),
            dma((3,)),
            dma((2, INNER)),
            dma((2, INNER)),
            dma((2, outer)),
            dma((2, outer)),
            dma((2, INNER)),
            dma((2, INNER)),
            dma((2,)),
            dma((2,)),
        ],
        compiler_params=pltpu.CompilerParams(
            collective_id=0, has_side_effects=True, vmem_limit_bytes=60 * 1024 * 1024
        ),
    )(features, cotangent, domain, qkv_weight, proj_weight, norm_gain[None, :])
    outs = pl.pallas_call(
        finish,
        out_shape=(
            jax.ShapeDtypeStruct(features.shape, BF16),
            jax.ShapeDtypeStruct(features.shape, BF16),
            jax.ShapeDtypeStruct((channels, 3 * channels), F32),
            jax.ShapeDtypeStruct((channels, channels), F32),
            jax.ShapeDtypeStruct((1, channels), F32),
        ),
        in_specs=[aspec] * 4,
        out_specs=(aspec,) * 5,
        scratch_shapes=[
            vm(features.shape, BF16),
            vm(features.shape, BF16),
            vm((1, channels), F32),
            vm((2, 2, INNER, piece, wide + 128), BF16),
            vm((channels, 3 * channels), F32),
            vm((channels, channels), F32),
            dma((7,)),
            dma((5,)),
        ],
        compiler_params=pltpu.CompilerParams(vmem_limit_bytes=60 * 1024 * 1024),
    )(*results)
    return (outs[0], outs[1], outs[2], outs[3], outs[4].reshape(channels))


def solution(mesh):
    return jax.shard_map(
        on_device,
        mesh=mesh,
        in_specs=(
            P(("grp", "row"), "col", None),
            P(("grp", "row"), "col", None),
            P(("grp", "row"), "col"),
            P(),
            P(),
            P(),
        ),
        out_specs=(
            P(("grp", "row"), "col", None),
            P(("grp", "row"), "col", None),
            P("grp", None),
            P("grp", None),
            P("grp"),
        ),
        check_vma=False,
    )
```

```python
import functools

import jax
import jax.numpy as jnp
from jax import lax
from jax.experimental import pallas as pl
from jax.experimental.pallas import tpu as pltpu
from jax.sharding import PartitionSpec as P

HEADS = 8
WIN = 8
SHIFT = 4
NORM_EPSILON = 1e-05
MASKED_SCORE = -1e30
LOG2E = 1.4426950408889634
INNER = 8
PAD = 16

F32 = jnp.float32
BF16 = jnp.bfloat16


def nn(a, b):
    return lax.dot_general(a, b, (((1,), (0,)), ((), ())), preferred_element_type=F32)


def nt(a, b):
    return lax.dot_general(a, b, (((1,), (1,)), ((), ())), preferred_element_type=F32)


def tn(a, b):
    return lax.dot_general(a, b, (((0,), (0,)), ((), ())), preferred_element_type=F32)


def kernel(
    rows,
    cols,
    feat_hbm,
    cot_hbm,
    dom_hbm,
    wqkv_hbm,
    wproj_hbm,
    gain_hbm,
    upd_hbm,
    gfeat_hbm,
    gsum_hbm,
    ggain_hbm,
    upd_ref,
    gfeat_ref,
    gsum_ref,
    ggain_ref,
    wqkv_ref,
    wproj_ref,
    gain_ref,
    dom_ref,
    dom_out,
    own,
    ext,
    ext_d,
    xf,
    cf,
    dx,
    mask,
    xhat,
    rstd,
    shifted,
    datt,
    proj,
    dproj,
    ctx,
    dctx,
    out32,
    outx,
    row_in,
    col_in,
    own_part,
    core_out,
    core_in,
    gcore_out,
    gcore_in,
    sbuf,
    rbuf,
    obuf,
    oin,
    local_sem,
    done_sem,
    in_send,
    in_recv,
    out_send,
    out_recv,
    core_send,
    core_recv,
    rs_send,
    rs_recv,
    o_send,
    o_recv,
    ag_send,
    ag_recv,
    fw_send,
    fw_recv,
):
    tile_rows, tile_cols, channels = feat_hbm.shape
    windows = tile_cols // WIN
    cells = WIN * WIN
    head_dim = channels // HEADS
    blocks = tile_cols // PAD
    chunks = 4
    each = windows // chunks
    reach = blocks // chunks
    outer = rows // INNER
    me_r = lax.axis_index("row")
    me_c = lax.axis_index("col")
    r_up = lax.rem(me_r + rows - 1, rows)
    r_dn = lax.rem(me_r + 1, rows)
    c_left = lax.rem(me_c + cols - 1, cols)
    c_right = lax.rem(me_c + 1, cols)
    group = me_r // INNER
    member = lax.rem(me_r, INNER)

    def dev(r, c):
        return {"row": r, "col": c}

    def peer(o):
        return group * INNER + lax.rem(member + o, INNER)

    def counterpart(o):
        return lax.rem(group + o, outer) * INNER + member

    barrier = pltpu.get_barrier_semaphore()
    greeted = [
        dev(r_up, me_c),
        dev(r_dn, me_c),
        dev(me_r, c_left),
        dev(r_up, c_left),
        dev(r_dn, c_right),
    ]
    greeted += [dev(peer(o), me_c) for o in range(1, INNER)]
    greeted += [dev(counterpart(o), me_c) for o in range(1, outer)]
    for target in greeted:
        pl.semaphore_signal(barrier, inc=1, device_id=target, device_id_type=pl.DeviceIdType.MESH)

    top, low = pl.ds(0, SHIFT), pl.ds(SHIFT, SHIFT)
    body, side, head = pl.ds(0, tile_cols), pl.ds(tile_cols, PAD), pl.ds(0, PAD)
    local = [
        pltpu.make_async_copy(s, d, local_sem.at[i])
        for i, (s, d) in enumerate(
            (
                (dom_hbm, dom_ref),
                (feat_hbm, own.at[0]),
                (cot_hbm, own.at[1]),
                (gain_hbm, gain_ref),
                (wqkv_hbm, wqkv_ref),
                (wproj_hbm, wproj_ref),
            )
        )
    ]
    for copy in local:
        copy.start()
    out32[:, :, 0:8, :] = jnp.zeros((2, tile_rows, 8, channels), F32)
    out32[:, :, tile_cols : tile_cols + PAD, :] = jnp.zeros((2, tile_rows, PAD, channels), F32)
    local[0].wait()
    dom = dom_ref[...].astype(F32)
    dom_out[...] = jnp.concatenate([dom, dom], 1)
    for copy in local[1:3]:
        copy.wait()
    pl.semaphore_wait(barrier, len(greeted))

    def remote(src, dst, send, recv, target):
        return pltpu.make_async_remote_copy(
            src_ref=src,
            dst_ref=dst,
            send_sem=send,
            recv_sem=recv,
            device_id=target,
            device_id_type=pl.DeviceIdType.MESH,
        )

    up, left, corner = dev(r_up, me_c), dev(me_r, c_left), dev(r_up, c_left)
    both = pl.ds(0, 2)
    jobs = [(dom_out, ext_d.at[i], t) for i, t in enumerate((up, left, corner))]
    cuts = [0] + [(b * reach + 1) * PAD for b in range(1, chunks)] + [tile_cols]
    for first, end in zip(cuts, cuts[1:]):
        if first < end:
            area = pl.ds(first, end - first)
            jobs.append((own.at[both, top, area], ext.at[both, low, area], up))
    jobs.append((own.at[both, low, head], ext.at[both, top, side], left))
    halos = [
        remote(s, d, in_send.at[i], in_recv.at[i], t) for i, (s, d, t) in enumerate(jobs)
    ]
    for copy in halos:
        copy.start()
    xf[0:SHIFT, 0:tile_cols, :] = own[0, SHIFT:, :, :].astype(F32)
    cf[0:SHIFT, 0:tile_cols, :] = own[1, SHIFT:, :, :].astype(F32)
    for copy in local[3:]:
        copy.wait()
    gain = gain_ref[...]

    scale = head_dim ** (-0.5)
    half = 128
    per = half // head_dim
    hid = lax.broadcasted_iota(jnp.int32, (per, 1, half), 0)
    lid = lax.broadcasted_iota(jnp.int32, (per, 1, half), 2) // head_dim
    hm32 = jnp.where(hid == lid, 1.0, 0.0).astype(F32)
    hm = hm32.astype(BF16)
    kid = lax.broadcasted_iota(jnp.int32, (cells, cells), 0)
    qid = lax.broadcasted_iota(jnp.int32, (cells, cells), 1)
    mid = WIN * SHIFT
    row_diff = jnp.where((kid >= mid) != (qid >= mid), MASKED_SCORE, 0.0)
    kcol, qcol = lax.rem(kid, WIN) >= SHIFT, lax.rem(qid, WIN) >= SHIFT
    col_diff = jnp.where(kcol != qcol, MASKED_SCORE, 0.0)
    row_bias = row_diff * jnp.where(me_r == rows - 1, 1.0, 0.0)
    last_bias = row_bias + col_diff * jnp.where(me_c == cols - 1, 1.0, 0.0)

    for copy in halos[0:3]:
        copy.wait()
    lane = lax.broadcasted_iota(jnp.int32, (SHIFT, 2 * tile_cols), 1)
    dx[0:SHIFT, :] = jnp.where(lane < tile_cols, dom_out[SHIFT:, :], ext_d[1, SHIFT:, :])
    dx[SHIFT:, :] = jnp.where(lane < tile_cols, ext_d[0, 0:SHIFT, :], ext_d[2, 0:SHIFT, :])
    pick = lax.broadcasted_iota(jnp.int32, (WIN, 2 * tile_cols), 1) - lax.broadcasted_iota(
        jnp.int32, (WIN, 2 * tile_cols), 0
    )

    def attend(ws, t):
        at = slice(t * half, (t + 1) * half)
        k_at = slice(channels + t * half, channels + (t + 1) * half)
        v_at = slice(2 * channels + t * half, 2 * channels + (t + 1) * half)
        heads = (per, cells, cells)
        flat = (per * cells, cells)
        kx = [(proj[w, :, k_at][None] * hm).reshape(per * cells, half) for w in ws]
        vx = [(proj[w, :, v_at][None] * hm).reshape(per * cells, half) for w in ws]
        s = [nt(k, proj[w, :, at]).reshape(heads) for k, w in zip(kx, ws)]
        dp = [nt(v, dctx[w, :, at]).astype(BF16).astype(F32).reshape(heads) for v, w in zip(vx, ws)]
        s = [x + (last_bias if w == windows - 1 else row_bias)[None] for x, w in zip(s, ws)]
        e = [jnp.exp2((x - jnp.max(x, 1, keepdims=True)) * (scale * LOG2E)) for x in s]
        p = [x * (1.0 / jnp.sum(x, 1, keepdims=True)) for x in e]
        pb = [x.astype(BF16).reshape(flat) for x in p]
        ds = [x * (y - jnp.sum(x * y, 1, keepdims=True)) for x, y in zip(p, dp)]
        dsb = [x.astype(BF16).reshape(flat) for x in ds]
        for n, w in enumerate(ws):
            ctx[w, :, at] = tn(pb[n], vx[n]).astype(BF16)
        for n, w in enumerate(ws):
            dv = nn(pb[n], dctx[w, :, at]).reshape(per, cells, half) * hm32
            dproj[w, :, v_at] = jnp.sum(dv, 0).astype(BF16)
        for n, w in enumerate(ws):
            dproj[w, :, at] = (tn(dsb[n], kx[n]) * scale).astype(BF16)
        for n, w in enumerate(ws):
            dk = nn(dsb[n], proj[w, :, at]).reshape(per, cells, half) * hm32
            dproj[w, :, k_at] = (jnp.sum(dk, 0) * scale).astype(BF16)

    gsum = jnp.zeros((WIN, channels), F32)
    outs = []
    for b in range(chunks):
        if cuts[b] < cuts[b + 1]:
            halos[3 + b].wait()
            block = slice(cuts[b], cuts[b + 1])
            xf[SHIFT:, block, :] = ext[0, SHIFT:, block, :].astype(F32)
            cf[SHIFT:, block, :] = ext[1, SHIFT:, block, :].astype(F32)
        if b == 0:
            at = len(jobs)
            passed = remote(
                ext.at[both, low, head], ext.at[both, low, side], in_send.at[at], in_recv.at[at], left
            )
            passed.start()
        if b == chunks - 1:
            halos[-1].wait()
            passed.wait()
            block = slice(tile_cols, tile_cols + PAD)
            xf[:, block, :] = ext[0, :, block, :].astype(F32)
            cf[:, block, :] = ext[1, :, block, :].astype(F32)
        mine_w = range(b * each, (b + 1) * each)
        for w in mine_w:
            for i in range(tile_rows):
                line = jnp.broadcast_to(dx[i : i + 1, :], (WIN, 2 * tile_cols))
                mask[w, i * WIN : (i + 1) * WIN, :] = jnp.sum(
                    jnp.where(pick == w * WIN + SHIFT, line, 0.0), -1, keepdims=True
                )
            at = slice(w * WIN + SHIFT, (w + 1) * WIN + SHIFT)
            x = xf[:, at, :].reshape(cells, channels)
            average = jnp.mean(x, -1, keepdims=True)
            centred = x - average
            variance = jnp.mean(centred * centred, -1, keepdims=True)
            inv = lax.rsqrt(variance + NORM_EPSILON)
            standard = centred * inv
            rstd[w] = inv
            xhat[w] = standard
            shifted[w] = (standard * gain).astype(BF16)
            c = cf[:, at, :].reshape(cells, channels)
            datt[w] = (c * mask[w]).astype(BF16)
        ws = slice(b * each, (b + 1) * each)
        count = each * cells
        s_chunk = shifted[ws].reshape(count, channels)
        d_chunk = datt[ws].reshape(count, channels)
        proj[ws] = nn(s_chunk, wqkv_ref[...]).astype(BF16).reshape(each, cells, 3 * channels)
        dctx[ws] = nt(d_chunk, wproj_ref[...]).astype(BF16).reshape(each, cells, channels)
        attend(mine_w, 0)

    total = windows * cells
    hrows = channels // 2
    share = hrows // INNER
    wide = 4 * half
    other = dev(me_r, c_right)

    def half_sum(core, t):
        at = pl.ds(pl.multiple_of(core * hrows, hrows), hrows)
        left_s = shifted[:, :, at].reshape(total, hrows)
        right_d = datt[:, :, at].reshape(total, hrows)
        heads = [
            dproj[:, :, n * channels + t * half : n * channels + (t + 1) * half].reshape(total, half)
            for n in range(3)
        ]
        left_c = ctx[:, :, t * half : (t + 1) * half].reshape(total, half)
        return tn(left_s, jnp.concatenate(heads, 1)), tn(left_c, right_d)

    def core_start(t):
        sum_q, sum_p = half_sum(c_right, t)
        core_out[t, :, 0 : 3 * half] = sum_q.astype(BF16)
        core_out[t, :, 3 * half :] = sum_p.astype(BF16)
        copy = remote(core_out.at[t], core_in.at[t], core_send.at[t], core_recv.at[t], other)
        copy.start()
        sum_q, sum_p = half_sum(me_c, t)
        own_part[t, :, 0 : 3 * half] = sum_q
        own_part[t, :, 3 * half :] = sum_p
        return copy

    def chip_sum(j, t):
        at = pl.ds(pl.multiple_of(j * share, share), share)
        sbuf[t, j, :, 0:wide] = (own_part[t, at, :] + core_in[t, at, :].astype(F32)).astype(BF16)

    def scatter_start(t):
        copies = [None]
        for o in range(1, INNER):
            j = lax.rem(member + o, INNER)
            chip_sum(j, t)
            copy = remote(
                sbuf.at[t, j],
                rbuf.at[t, o],
                rs_send.at[t, o],
                rs_recv.at[t, o],
                dev(peer(o), me_c),
            )
            copy.start()
            copies.append(copy)
        chip_sum(member, t)
        return copies

    def scatter_end(t, copies):
        acc = sbuf[t, member].astype(F32)
        for o in range(1, INNER):
            copies[o].wait()
            acc = acc + rbuf[t, o].astype(F32)
        return acc

    def gather_start(t, acc, extra):
        acc = jnp.concatenate([acc, extra], 1)
        if outer > 1:
            obuf[t] = acc.astype(BF16)
            spread = [
                remote(
                    obuf.at[t],
                    oin.at[t, o],
                    o_send.at[t, o],
                    o_recv.at[t, o],
                    dev(counterpart(o), me_c),
                )
                for o in range(1, outer)
            ]
            for copy in spread:
                copy.start()
            for o in range(1, outer):
                spread[o - 1].wait()
                acc = acc + oin[t, o].astype(F32)
        mine = gsum_ref.at[t, me_c, member]
        mine[...] = acc.astype(BF16)
        copies = [
            remote(mine, mine, ag_send.at[t, o], ag_recv.at[t, o], dev(peer(o), me_c))
            for o in range(1, INNER)
        ]
        for copy in copies:
            copy.start()
        return copies

    def gather_end(t, copies):
        for copy in copies:
            copy.wait()
        column = gsum_ref.at[t, me_c]
        copy = remote(column, column, fw_send.at[t], fw_recv.at[t], other)
        copy.start()
        return copy

    early = core_start(0)
    for b in range(chunks):
        ws = slice(b * each, (b + 1) * each)
        mine_w = range(b * each, (b + 1) * each)
        attend(mine_w, 1)
        if b == 0:
            early.wait()
            early_scatter = scatter_start(0)
        if b == chunks - 2:
            acc = scatter_end(0, early_scatter)
            early_gather = gather_start(0, acc, jnp.zeros((share, 128), F32))
        if b == chunks - 1:
            late = core_start(1)
        p_chunk = dproj[ws].reshape(count, 3 * channels)
        dnormed = nt(p_chunk, wqkv_ref[...]).astype(BF16).astype(F32)
        c_chunk = ctx[ws].reshape(count, channels)
        attended = nn(c_chunk, wproj_ref[...]).astype(BF16).astype(F32)
        for u, w in enumerate(mine_w):
            at = slice(w * WIN + SHIFT, (w + 1) * WIN + SHIFT)
            dn = dnormed[u * cells : (u + 1) * cells]
            standard = xhat[w]
            gsum = gsum + jnp.sum((dn * standard).reshape(WIN, WIN, channels), 0)
            up_grad = dn * gain
            mean_g = jnp.mean(up_grad, -1, keepdims=True)
            mean_gx = jnp.mean(up_grad * standard, -1, keepdims=True)
            grad = rstd[w] * (up_grad - mean_g - standard * mean_gx)
            out32[1, :, at, :] = cf[:, at, :] + grad.reshape(WIN, WIN, channels)
            inside = mask[w] * attended[u * cells : (u + 1) * cells]
            out32[0, :, at, :] = xf[:, at, :] + inside.reshape(WIN, WIN, channels)
        block = slice(b * reach * PAD, (b + 1) * reach * PAD)
        outx[:, :, block, :] = out32[:, :, block, :].astype(BF16)
        first = max(b * reach, 1) * PAD
        area = pl.ds(first, (b + 1) * reach * PAD - first)
        if first < (b + 1) * reach * PAD:
            copy = remote(
                outx.at[both, low, area],
                row_in.at[both, top, area],
                out_send.at[b],
                out_recv.at[b],
                dev(r_dn, me_c),
            )
            copy.start()
            outs.append(copy)

    edge = slice(tile_cols, tile_cols + PAD)
    outx[:, :, edge, :] = out32[:, :, edge, :].astype(BF16)
    aside = remote(
        outx.at[both, pl.ds(0, tile_rows), side],
        col_in,
        out_send.at[blocks],
        out_recv.at[blocks],
        dev(me_r, c_right),
    )
    aside.start()
    late.wait()
    late_scatter = scatter_start(1)
    gtile = jnp.concatenate([gsum[:, :half], gsum[:, half:]], 0)
    gcore_out[...] = gtile.astype(BF16)
    gain_copy = remote(gcore_out, gcore_in, core_send.at[2], core_recv.at[2], other)
    gain_copy.start()
    aside.wait()
    col_id = lax.broadcasted_iota(jnp.int32, (tile_rows, PAD, channels), 1)
    for n in range(2):
        outx[n, :, 0:PAD, :] = jnp.where(
            col_id < SHIFT, col_in[n].astype(F32), outx[n, :, 0:PAD, :].astype(F32)
        ).astype(BF16)
    copy = remote(
        outx.at[both, low, head],
        row_in.at[both, top, head],
        out_send.at[blocks + 1],
        out_recv.at[blocks + 1],
        dev(r_dn, me_c),
    )
    copy.start()
    outs.append(copy)
    early_hand = gather_end(0, early_gather)
    gain_copy.wait()
    gchip = gtile + gcore_in[...].astype(F32)
    late_gather = gather_start(1, scatter_end(1, late_scatter), gchip)

    def give(i, src, dst):
        copy = pltpu.make_async_copy(src, dst, done_sem.at[i])
        copy.start()
        return copy

    results = []
    for copy in outs:
        copy.wait()
    for n, ref in enumerate((upd_ref, gfeat_ref)):
        ref[0:SHIFT, :, :] = row_in[n]
        ref[SHIFT:, :, :] = outx[n, 0:SHIFT, 0:tile_cols, :]
    results += [give(1, upd_ref, upd_hbm), give(2, gfeat_ref, gfeat_hbm)]

    late_hand = gather_end(1, late_gather)
    results.append(give(3, gsum_ref.at[both, me_c], gsum_hbm.at[both, me_c]))
    gains = jnp.sum(gsum_ref[1, me_c, :, :, wide:].astype(F32), 0)
    gfold = jnp.concatenate([gains[0:WIN], gains[WIN:]], 1)
    ggain_ref[...] = jnp.sum(gfold, 0, keepdims=True)
    results.append(give(0, ggain_ref, ggain_hbm))
    early_hand.wait()
    late_hand.wait()
    results.append(give(4, gsum_ref.at[both, c_right], gsum_hbm.at[both, c_right]))
    for copy in results:
        copy.wait()


def finish(
    upd_in,
    gfeat_in,
    gsum_in,
    ggain_in,
    upd,
    gfeat,
    gqkv,
    gproj,
    ggain,
    upd_mid,
    gfeat_mid,
    ggain_mid,
    sums,
    qkv32,
    proj32,
    in_sems,
    out_sems,
):
    channels = gqkv.shape[0]
    parts, halves, _, _, wide = sums.shape
    hrows = channels // halves
    half = 128
    pairs = [(t, c) for t in range(parts) for c in range(halves)]

    def copies(jobs, sems):
        return [pltpu.make_async_copy(s, d, sems.at[i]) for i, (s, d) in enumerate(jobs)]

    reads = [(gsum_in.at[t, c], sums.at[t, c]) for t, c in pairs]
    reads += [(upd_in, upd_mid), (gfeat_in, gfeat_mid), (ggain_in, ggain_mid)]
    writes = [(qkv32, gqkv), (proj32, gproj)]
    writes += [(upd_mid, upd), (gfeat_mid, gfeat), (ggain_mid, ggain)]
    reads, writes = copies(reads, in_sems), copies(writes, out_sems)
    for copy in reads:
        copy.start()
    for n, (t, c) in enumerate(pairs):
        reads[n].wait()
        some = sums[t, c].reshape(hrows, wide).astype(F32)
        rows = slice(c * hrows, (c + 1) * hrows)
        for n in range(3):
            at = slice(n * channels + t * half, n * channels + (t + 1) * half)
            qkv32[rows, at] = some[:, n * half : (n + 1) * half]
        proj32[t * half : (t + 1) * half, rows] = some[:, 3 * half : 4 * half]
    for n in range(2):
        writes[n].start()
    for n in range(3):
        reads[len(pairs) + n].wait()
        writes[2 + n].start()
    for copy in writes:
        copy.wait()


def on_device(features, cotangent, domain, qkv_weight, proj_weight, norm_gain):
    tile_rows, tile_cols, channels = features.shape
    rows, cols = lax.axis_size("row"), lax.axis_size("col")
    outer = rows // INNER
    windows, cells = tile_cols // WIN, WIN * WIN
    blocks = tile_cols // PAD
    piece = channels // 2 // INNER
    wide = 4 * 128
    ext = tile_cols + PAD
    vm = pltpu.VMEM
    dma = pltpu.SemaphoreType.DMA
    halos = 3 + blocks + 2
    aspec = pl.BlockSpec(memory_space=pltpu.HBM)
    results = pl.pallas_call(
        functools.partial(kernel, rows, cols),
        out_shape=(
            jax.ShapeDtypeStruct(features.shape, BF16),
            jax.ShapeDtypeStruct(features.shape, BF16),
            jax.ShapeDtypeStruct((2, 2, INNER, piece, wide + 128), BF16),
            jax.ShapeDtypeStruct((1, channels), F32),
        ),
        in_specs=[aspec] * 6,
        out_specs=(aspec,) * 4,
        scratch_shapes=[
            vm(features.shape, BF16),
            vm(features.shape, BF16),
            vm((2, 2, INNER, piece, wide + 128), BF16),
            vm((1, channels), F32),
            vm(qkv_weight.shape, BF16),
            vm(proj_weight.shape, BF16),
            vm((1, channels), F32),
            vm((tile_rows, tile_cols), jnp.int32),
            vm((tile_rows, 2 * tile_cols), F32),
            vm((2, tile_rows, tile_cols, channels), BF16),
            vm((2, tile_rows, ext, channels), BF16),
            vm((3, tile_rows, 2 * tile_cols), F32),
            vm((tile_rows, ext, channels), F32),
            vm((tile_rows, ext, channels), F32),
            vm((tile_rows, 2 * tile_cols), F32),
            vm((windows, cells, 1), F32),
            vm((windows, cells, channels), F32),
            vm((windows, cells, 1), F32),
            vm((windows, cells, channels), BF16),
            vm((windows, cells, channels), BF16),
            vm((windows, cells, 3 * channels), BF16),
            vm((windows, cells, 3 * channels), BF16),
            vm((windows, cells, channels), BF16),
            vm((windows, cells, channels), BF16),
            vm((2, tile_rows, ext, channels), F32),
            vm((2, tile_rows, ext, channels), BF16),
            vm((2, SHIFT, tile_cols, channels), BF16),
            vm((2, tile_rows, PAD, channels), BF16),
            vm((2, channels // 2, wide), F32),
            vm((2, channels // 2, wide), BF16),
            vm((2, channels // 2, wide), BF16),
            vm((16, 128), BF16),
            vm((16, 128), BF16),
            vm((2, INNER, piece, wide), BF16),
            vm((2, INNER, piece, wide), BF16),
            vm((2, piece, wide + 128), BF16),
            vm((2, outer, piece, wide + 128), BF16),
            dma((6,)),
            dma((5,)),
            dma((halos,)),
            dma((halos,)),
            dma((blocks + 2,)),
            dma((blocks + 2,)),
            dma((3,)),
            dma((3,)),
            dma((2, INNER)),
            dma((2, INNER)),
            dma((2, outer)),
            dma((2, outer)),
            dma((2, INNER)),
            dma((2, INNER)),
            dma((2,)),
            dma((2,)),
        ],
        compiler_params=pltpu.CompilerParams(
            collective_id=0, has_side_effects=True, vmem_limit_bytes=60 * 1024 * 1024
        ),
    )(features, cotangent, domain, qkv_weight, proj_weight, norm_gain[None, :])
    outs = pl.pallas_call(
        finish,
        out_shape=(
            jax.ShapeDtypeStruct(features.shape, BF16),
            jax.ShapeDtypeStruct(features.shape, BF16),
            jax.ShapeDtypeStruct((channels, 3 * channels), F32),
            jax.ShapeDtypeStruct((channels, channels), F32),
            jax.ShapeDtypeStruct((1, channels), F32),
        ),
        in_specs=[aspec] * 4,
        out_specs=(aspec,) * 5,
        scratch_shapes=[
            vm(features.shape, BF16),
            vm(features.shape, BF16),
            vm((1, channels), F32),
            vm((2, 2, INNER, piece, wide + 128), BF16),
            vm((channels, 3 * channels), F32),
            vm((channels, channels), F32),
            dma((7,)),
            dma((5,)),
        ],
        compiler_params=pltpu.CompilerParams(vmem_limit_bytes=60 * 1024 * 1024),
    )(*results)
    return (outs[0], outs[1], outs[2], outs[3], outs[4].reshape(channels))


def solution(mesh):
    return jax.shard_map(
        on_device,
        mesh=mesh,
        in_specs=(
            P(("grp", "row"), "col", None),
            P(("grp", "row"), "col", None),
            P(("grp", "row"), "col"),
            P(),
            P(),
            P(),
        ),
        out_specs=(
            P(("grp", "row"), "col", None),
            P(("grp", "row"), "col", None),
            P("grp", None),
            P("grp", None),
            P("grp"),
        ),
        check_vma=False,
    )
```
